128 devices in a mesh: px: 8 (over z_lo, y), py: 16 (over z_hi, x, core).
Axes of the slice: x: 4, y: 4, z: 4 (z_hi: 2, z_lo: 2; z = z_hi * 2 + z_lo), core: 2. Of those that a mesh axis runs over, the one named last changes fastest.
Arguments:
- velocity: float32 [3, 32, 256, 512], P(None, 'px', 'py'), may hold values from -4 to 4
- first_weight: bfloat16 [64, 81], replicated, may hold values from -0.625 to 0.625
- mid_weight: bfloat16 [64, 64], replicated, may hold values from -0.75 to 0.75
- last_weight: bfloat16 [6, 64], replicated, may hold values from -0.75 to 0.75
- offsets: int32 [32, 256], P('px', 'py'), may hold values from 0 to 256
Outputs:
- final_velocity: float32 [3, 32, 256, 512], P(None, 'px', 'py')
- grad_first: float32 [64, 81], replicated
- grad_mid: float32 [64, 64], replicated
- grad_last: float32 [6, 64], replicated
The draws below stay inside these ranges and needn't reach their ends.
All inputs are finite; a program needn't handle non-finite values.
Results may differ from the reference program's by a relative error of at most 0.0003.
Values may be sent and summed in bfloat16 or wider, within the bound.
No kernel may reach another device: no remote copies, remote signals or barrier semaphores. Data moves between devices by JAX's collectives and lax.ppermute only.
A program may use at most 192 MiB of HBM per device.

```python
import jax
import jax.numpy as jnp
from jax import lax

NZ = 512
HID = 64
WINDOW = 256
NX = 32
NY = 256


def with_ends(result, stream_key, smallest, top_value):
    index_at = [jax.random.randint(jax.random.fold_in(stream_key, axis), (), 0, length) for axis, length in enumerate(result.shape)]
    longest = result.shape.index(max(result.shape))
    next_to = index_at[:longest] + [(index_at[longest] + 1) % result.shape[longest]] + index_at[longest + 1:]
    return result.at[tuple(index_at)].set(smallest).at[tuple(next_to)].set(top_value)


def levels(own_key, extent, cuts, least, largest):
    gain, own = 1.0, jax.random.fold_in(own_key, 6)
    for dim, blocks in cuts:
        draws = jnp.exp(jax.random.uniform(jax.random.fold_in(own, dim), (blocks,), jnp.float32, least / len(cuts), largest / len(cuts)))
        gain = gain * jnp.repeat(draws, extent[dim] // blocks).reshape([-1 if axis == dim else 1 for axis in range(len(extent))])
    return gain


def scatter_about(stream_key, dims, spread, limit, split=(), kind=jnp.bfloat16):
    result = spread * jax.random.normal(stream_key, dims, jnp.float32)
    if split:
        result = result * levels(stream_key, dims, split, -0.22, 0.18)
    return jnp.clip(result, -limit, limit).astype(kind)


def setup_inputs(seed: int = 0) -> dict:
    seeds = jax.random.split(jax.random.key(seed), 6)
    return {
        "velocity": scatter_about(seeds[0], (3, NX, NY, NZ), 1.0, 4.0, ((1, 8), (2, 16)), jnp.float32),
        "first_weight": scatter_about(seeds[1], (HID, 81), 81 ** -0.5, 0.625),
        "mid_weight": scatter_about(seeds[2], (HID, HID), HID ** -0.5, 0.75),
        "last_weight": scatter_about(seeds[3], (6, HID), HID ** -0.5, 0.75),
        "offsets": with_ends(jax.random.randint(seeds[4], (NX, NY), 0, NZ - WINDOW + 1), jax.random.fold_in(seeds[4], 1), 0, NZ - WINDOW).astype(jnp.int32),
    }


time_step = 0.1
viscosity = 0.05
smagorinsky = 0.04
forcing = 0.05
pair_list = ((0, 0), (1, 1), (2, 2), (0, 1), (0, 2), (1, 2))

def derive(field_in, dimension):
    middle = [slice(None), slice(1, -1), slice(1, -1), slice(1, -1)]
    upper_cut = list(middle)
    lower_cut = list(middle)
    upper_cut[dimension] = slice(2, None)
    lower_cut[dimension] = slice(None, -2)
    return 0.5 * (field_in[tuple(upper_cut)] - field_in[tuple(lower_cut)])

def pair_index(row_index, col_index):
    return pair_list.index((min(row_index, col_index), max(row_index, col_index)))

def advance(extended):
    padded = jnp.pad(extended, ((0, 0), (0, 0), (0, 0), (2, 2)))
    gradient = [derive(padded, dimension) for dimension in (1, 2, 3)]
    strain = jnp.stack([0.5 * (gradient[row_index][col_index] + gradient[col_index][row_index]) for row_index, col_index in pair_list])
    squares = strain[0] ** 2 + strain[1] ** 2 + strain[2] ** 2 + 2.0 * (strain[3] ** 2 + strain[4] ** 2 + strain[5] ** 2)
    eddy_visc = viscosity + smagorinsky * jnp.sqrt(2.0 * squares)
    stress = -2.0 * eddy_visc[None] * strain
    center = padded[:, 2:-2, 2:-2, 2:-2]
    updated = []
    for component in range(3):
        stress_div = sum((derive(stress[pair_index(dimension, component)][None], dimension + 1)[0] for dimension in range(3)))
        advect = sum((center[dimension] * gradient[dimension][component][1:-1, 1:-1, 1:-1] for dimension in range(3)))
        source = forcing if component == 0 else 0.0
        updated.append(center[component] + time_step * (source - advect - stress_div))
    return (jnp.stack(updated), stress[:, 1:-1, 1:-1, 1:-1])

def silu_slope(hidden_in):
    sigmoid = jax.nn.sigmoid(hidden_in)
    return sigmoid * (1.0 + hidden_in * (1.0 - sigmoid))

def columns_of(extended):
    length_x = extended.shape[1] - 2
    length_y = extended.shape[2] - 2
    length_z = extended.shape[3] - 2
    pieces = [extended[channel, offset_x:offset_x + length_x, offset_y:offset_y + length_y, offset_z:offset_z + length_z] for channel in range(3) for offset_x in range(3) for offset_y in range(3) for offset_z in range(3)]
    return jnp.stack(pieces).reshape(len(pieces), -1)

def contract_cells(left_side, right_side):
    return lax.dot_general(left_side, right_side, (((1,), (1,)), ((), ())), preferred_element_type=jnp.float32)

def contract_rows(left_side, right_side):
    return lax.dot_general(left_side, right_side, (((0,), (0,)), ((), ())), preferred_element_type=jnp.float32)

def closure_grads(columns, target, cell_mask, first_weight, mid_weight, last_weight):
    hidden_one = jnp.dot(first_weight, columns, preferred_element_type=jnp.float32)
    active_one = jax.nn.silu(hidden_one).astype(jnp.bfloat16)
    hidden_two = jnp.dot(mid_weight, active_one, preferred_element_type=jnp.float32)
    active_two = jax.nn.silu(hidden_two).astype(jnp.bfloat16)
    predicted = jnp.dot(last_weight, active_two, preferred_element_type=jnp.float32)
    misfit = ((predicted - target.astype(jnp.float32)) * cell_mask).astype(jnp.bfloat16)
    grad_last = contract_cells(misfit, active_two)
    back_two = (contract_rows(last_weight, misfit) * silu_slope(hidden_two)).astype(jnp.bfloat16)
    grad_mid = contract_cells(back_two, active_one)
    back_one = (contract_rows(mid_weight, back_two) * silu_slope(hidden_one)).astype(jnp.bfloat16)
    grad_first = contract_cells(back_one, columns)
    return (grad_first, grad_mid, grad_last)

def window_test(offset_rows, heights, window_len):
    lowest = offset_rows[..., None]
    return jnp.logical_and(heights >= lowest, heights < lowest + window_len).astype(jnp.float32)

def reference(velocity, first_weight, mid_weight, last_weight, offsets):
    wrap_pad = ((0, 0), (2, 2), (2, 2), (0, 0))
    middle_vel, stress_zero = advance(jnp.pad(velocity, wrap_pad, mode='wrap'))
    final_vel, stress_one = advance(jnp.pad(middle_vel, wrap_pad, mode='wrap'))
    totals = (jnp.zeros(first_weight.shape, jnp.float32), jnp.zeros(mid_weight.shape, jnp.float32), jnp.zeros(last_weight.shape, jnp.float32))
    block_rows = 8
    heights = jnp.arange(NZ, dtype=jnp.int32)
    for snapshot, stress in ((velocity, stress_zero), (middle_vel, stress_one)):
        inputs = jnp.pad(snapshot.astype(jnp.bfloat16), ((0, 0), (1, 1), (1, 1), (0, 0)), mode='wrap')
        inputs = jnp.pad(inputs, ((0, 0), (0, 0), (0, 0), (1, 1)))
        target = stress.astype(jnp.bfloat16)

        def body_block(block_index, carry):
            block_start = (block_index * block_rows).astype(jnp.int32)
            part_in = lax.dynamic_slice_in_dim(inputs, block_start, block_rows + 2, 1)
            part_tgt = lax.dynamic_slice_in_dim(target, block_start, block_rows, 1).reshape(6, -1)
            part_off = lax.dynamic_slice_in_dim(offsets, block_start, block_rows, 0)
            cell_mask = window_test(part_off, heights, WINDOW).reshape(-1)
            grads = closure_grads(columns_of(part_in), part_tgt, cell_mask, first_weight, mid_weight, last_weight)
            return tuple((total + extra for total, extra in zip(carry, grads)))
        totals = lax.fori_loop(0, NX // block_rows, body_block, totals)
    sample_count = float(2 * NX * NY * WINDOW)
    return (final_vel, totals[0] / sample_count, totals[1] / sample_count, totals[2] / sample_count)
```

```python
import jax
import jax.numpy as jnp
import numpy as np
from jax import lax
from jax.experimental import pallas as pl
from jax.experimental.pallas import tpu as pltpu
from jax.sharding import PartitionSpec as P

f32, bf16 = jnp.float32, jnp.bfloat16
AXES = ("px", "py")
LANES = 640
ROWS = 40
WINDOW = 256
NT = (((1,), (1,)), ((), ()))


def selections():
    pick = np.zeros((512, 216), np.float32)
    pick_target = np.zeros((256, 96), np.float32)
    for y in range(16):
        for c in range(3):
            for ox in range(3):
                for oy in range(3):
                    pick[y * 32 + c * 9 + ox * 3 + oy, (c * 3 + ox) * 24 + y + oy + 3] = 1
        for c in range(6):
            pick_target[y * 16 + c, c * 16 + y] = 1
    back = np.zeros((96, 128), np.float32)
    for oz in range(3):
        for c in range(3):
            for o in range(9):
                back[oz * 32 + c * 9 + o, c * 27 + o * 3 + oz] = 1
    return pick, pick_target, back


def dot(a, b):
    return jnp.dot(a, b, preferred_element_type=f32)


def dot_cells(a, b):
    return lax.dot_general(a, b, NT, preferred_element_type=f32)


def shift_z(value):
    return pltpu.roll(value, LANES - 1, 1) - pltpu.roll(value, 1, 1)


def differences(field, plane, row):
    here = pl.ds(row, 8)
    center = [field[c, plane, here, :] for c in range(3)]
    along_x = [field[c, plane + 1, here, :] - field[c, plane - 1, here, :] for c in range(3)]
    along_y = [field[c, plane, pl.ds(row + 1, 8), :] - field[c, plane, pl.ds(row - 1, 8), :] for c in range(3)]
    along_z = [shift_z(center[c]) for c in range(3)]
    return center, (along_x, along_y, along_z)


def stress_rows(field, plane, tau, tau_plane, row):
    _, d = differences(field, plane, row)
    xy, xz, yz = d[0][1] + d[1][0], d[0][2] + d[2][0], d[1][2] + d[2][1]
    diagonal = d[0][0] * d[0][0] + d[1][1] * d[1][1] + d[2][2] * d[2][2]
    mixed = xy * xy + xz * xz + yz * yz
    nu = 0.05 + 0.04 * jnp.sqrt(0.5 * diagonal + 0.25 * mixed)
    half = -0.5 * nu
    rows = pl.ds(row, 8)
    for c in range(3):
        tau[c, tau_plane, rows, :] = -nu * d[c][c]
    tau[3, tau_plane, rows, :] = half * xy
    tau[4, tau_plane, rows, :] = half * xz
    tau[5, tau_plane, rows, :] = half * yz


def step_rows(field, plane, tau, tau_plane, row):
    center, d = differences(field, plane, row)
    here = pl.ds(row, 8)

    def tau_x(c):
        return tau[c, tau_plane + 1, here, :] - tau[c, tau_plane - 1, here, :]

    def tau_y(c):
        return tau[c, tau_plane, pl.ds(row + 1, 8), :] - tau[c, tau_plane, pl.ds(row - 1, 8), :]

    def tau_z(c):
        return shift_z(tau[c, tau_plane, here, :])

    parts = ((0, 3, 4), (3, 1, 5), (4, 5, 2))
    out = []
    for j in range(3):
        a, b, c = parts[j]
        total = tau_x(a) + tau_y(b) + tau_z(c)
        total += center[0] * d[0][j] + center[1] * d[1][j] + center[2] * d[2][j]
        new = center[j] - 0.05 * total
        out.append(new + 0.005 if j == 0 else new)
    return out


def closure(field, base, tau, tau_base, offs, pick, pick_target, tile, tile_target, weights, totals):
    w1, w2, w2t, w3, w3t = weights
    g1, g2, g3 = totals

    def step(x, _):
        rows = [field[c, base + x + ox - 1, 8:32, 0:512] for c in range(3) for ox in range(3)]
        tile[:, 128:640] = dot(pick[...], jnp.concatenate(rows, 0).astype(bf16)).astype(bf16)
        rows = [tau[c, tau_base + x, 12:28, 0:512].astype(bf16) for c in range(6)]
        tile_target[:, 128:640] = dot(pick_target[...], jnp.concatenate(rows, 0)).astype(bf16)
        columns, targets = [], []
        for y in range(16):
            start = offs[x, y] + 127
            base_lane = pl.multiple_of(lax.shift_right_logical(start, 7) * 128, 128)
            turn = (512 - (start & 127)) & 511
            window = pltpu.roll(tile[y * 32 : y * 32 + 32, pl.ds(base_lane, 512)], turn, 1)
            columns.append(jnp.concatenate([window[:, 0:256], window[:, 1:257], window[:, 2:258]], 0))
            target = pltpu.roll(tile_target[y * 16 : y * 16 + 16, pl.ds(base_lane, 512)], turn, 1)
            targets.append(target[:, 1:257])
        cols = jnp.concatenate(columns, 1)
        target = jnp.concatenate(targets, 1)
        h1 = dot(w1[...], cols)
        t1 = jnp.tanh(h1)
        q1 = h1 * t1
        a1 = (h1 + q1).astype(bf16)
        s1 = (1.0 + t1) * (1.0 + (h1 - q1))
        h2 = dot(w2[...], a1)
        t2 = jnp.tanh(h2)
        q2 = h2 * t2
        a2 = (h2 + q2).astype(bf16)
        s2 = (1.0 + t2) * (1.0 + (h2 - q2))
        misfit = dot(w3[...], jnp.concatenate([a2, target], 0)).astype(bf16)
        b2 = (dot(w3t[...], misfit) * s2).astype(bf16)
        b1 = (dot(w2t[...], b2) * s1).astype(bf16)
        g3[...] += dot_cells(misfit, a2)
        g2[...] += dot_cells(b2, a1)
        g1[...] += dot_cells(b1, cols)
        return 0

    lax.fori_loop(0, 4, step, 0)


def kernel(
    offs, own, x_low, x_high, y_low, y_high, w1, w2, w2t, w3, w3t, pick, pick_target, back,
    final, packed, field, middle, tau, tile, tile_target, g1, g2, g3,
):
    zeros = jnp.zeros((ROWS, 128), f32)
    line = jnp.zeros((1, LANES), f32)
    for c in range(3):
        for p in range(12):
            field[c, p, :, 512:640] = zeros
            field[c, p, 7:8, :] = line
            field[c, p, 32:33, :] = line
            source, q = ((x_low, p), (own, p - 4), (x_high, p - 8))[p // 4]
            field[c, p, 12:28, 0:512] = source[c, q]
            field[c, p, 8:12, 0:512] = y_low[c, p]
            field[c, p, 28:32, 0:512] = y_high[c, p]
    for c in range(6):
        for p in range(10):
            tau[c, p, 7:8, :] = line
            tau[c, p, 32:33, :] = line
    for target in (tile, tile_target):
        edge = jnp.zeros((target.shape[0], 128), bf16)
        target[:, 0:128] = edge
        target[:, 640:768] = edge
    g1[...] = jnp.zeros_like(g1)
    g2[...] = jnp.zeros_like(g2)
    g3[...] = jnp.zeros_like(g3)
    weights, totals = (w1, w2, w2t, w3, w3t), (g1, g2, g3)

    def stress_zero(p, _):
        for row in (8, 16, 24):
            stress_rows(field, p + 1, tau, p, row)
        return 0

    lax.fori_loop(0, 10, stress_zero, 0)
    closure(field, 4, tau, 3, offs, pick, pick_target, tile, tile_target, weights, totals)

    inside = lax.broadcasted_iota(jnp.int32, (8, LANES), 1) < 512

    def advance_middle(p, _):
        for row in (8, 16, 24):
            new = step_rows(field, p + 2, tau, p + 1, row)
            for c in range(3):
                middle[c, p, pl.ds(row, 8), :] = jnp.where(inside, new[c], 0.0)
        return 0

    lax.fori_loop(0, 8, advance_middle, 0)

    def stress_one(p, _):
        for row in (8, 16, 24):
            stress_rows(middle, p + 1, tau, p, row)
        return 0

    lax.fori_loop(0, 6, stress_one, 0)
    closure(middle, 2, tau, 1, offs, pick, pick_target, tile, tile_target, weights, totals)

    def advance_final(p, _):
        for row in (12, 20):
            new = step_rows(middle, p + 2, tau, p + 1, row)
            for c in range(3):
                final[c, p, row - 12 : row - 4, :] = new[c][:, 0:512]
        return 0

    lax.fori_loop(0, 4, advance_final, 0)
    scale = 0.5**22
    packed[0:64, :] = scale * jnp.dot(
        g1[...], back[...], preferred_element_type=f32, precision=lax.Precision.HIGHEST
    )
    packed[64:96, :] = scale * jnp.concatenate([g2[0:32, :], g2[32:64, :]], 1)
    packed[96:104, :] = scale * jnp.concatenate([g3[0:8, :], jnp.zeros((8, 64), f32)], 1)


def run_kernel(offsets, own, x_low, x_high, y_low, y_high, w1, w2, w2t, w3, w3t):
    pick, pick_target, back = selections()
    vmem = pl.BlockSpec(memory_space=pltpu.VMEM)
    smem = pl.BlockSpec(memory_space=pltpu.SMEM)
    return pl.pallas_call(
        kernel,
        in_specs=[smem] + [vmem] * 13,
        out_specs=[vmem] * 2,
        out_shape=[
            jax.ShapeDtypeStruct((3, 4, 16, 512), f32),
            jax.ShapeDtypeStruct((104, 128), f32),
        ],
        scratch_shapes=[
            pltpu.VMEM((3, 12, ROWS, LANES), f32),
            pltpu.VMEM((3, 8, ROWS, LANES), f32),
            pltpu.VMEM((6, 10, ROWS, LANES), f32),
            pltpu.VMEM((512, 768), bf16),
            pltpu.VMEM((256, 768), bf16),
            pltpu.VMEM((64, 96), f32),
            pltpu.VMEM((64, 64), f32),
            pltpu.VMEM((16, 64), f32),
        ],
        compiler_params=pltpu.CompilerParams(vmem_limit_bytes=56 * 2**20),
    )(
        offsets, own, x_low, x_high, y_low, y_high, w1, w2, w2t, w3, w3t,
        jnp.asarray(pick, bf16), jnp.asarray(pick_target, bf16), jnp.asarray(back, f32),
    )


def pairs(move):
    return [(i * 16 + j, (move(i, j)[0] % 8) * 16 + move(i, j)[1] % 16) for i in range(8) for j in range(16)]


def partner(k, odd_up):
    if not odd_up:
        return k ^ 1
    return (k + 1) % 4 if k % 2 else (k - 1) % 4


def swap_core(i, j):
    return (i, j ^ 1)


def swap_y(odd_up):
    return lambda i, j: (i & 4 | partner(i & 3, odd_up), j)


def swap_x(odd_up):
    return lambda i, j: (i, j & 9 | partner(j >> 1 & 3, odd_up) << 1)


def swap_z(odd_up):
    def move(i, j):
        z = partner((j >> 3) * 2 + (i >> 2), odd_up)
        return ((z & 1) * 4 + (i & 3), (z >> 1) * 8 + (j & 7))

    return move


def sum_everywhere(value):
    for move in (swap_core, swap_y(0), swap_y(1), swap_x(0), swap_x(1), swap_z(0), swap_z(1)):
        value = value + lax.ppermute(value, AXES, pairs(move))
    return value


def body(velocity, first_weight, mid_weight, last_weight, offsets):
    up = pairs(lambda i, j: (i + 1, j))
    down = pairs(lambda i, j: (i - 1, j))
    x_low = lax.ppermute(velocity, AXES, up)
    x_high = lax.ppermute(velocity, AXES, down)
    wide = jnp.concatenate([x_low, velocity, x_high], 1)
    y_low = lax.ppermute(wide[:, :, 12:, :], AXES, pairs(lambda i, j: (i, j + 1)))
    y_high = lax.ppermute(wide[:, :, :4, :], AXES, pairs(lambda i, j: (i, j - 1)))

    half = jnp.asarray(0.5, bf16)
    w1 = jnp.transpose(first_weight.reshape(64, 27, 3), (0, 2, 1))
    w1 = (jnp.pad(w1, ((0, 0), (0, 0), (0, 5))) * half).reshape(64, 96)
    w2 = mid_weight * half
    w2t = mid_weight.T * half
    w3 = jnp.pad(last_weight, ((0, 10), (0, 0)))
    w3t = w3.T * half
    w3 = jnp.concatenate([w3, -jnp.eye(16, dtype=bf16)], 1)
    final, packed = run_kernel(offsets, velocity, x_low, x_high, y_low, y_high, w1, w2, w2t, w3, w3t)
    total = sum_everywhere(packed)
    grad_mid = jnp.concatenate([total[64:96, :64], total[64:96, 64:]], 0)
    return final, total[:64, :81], grad_mid, total[96:102, :64]


def solution(mesh):
    in_specs = (P(None, "px", "py", None), P(), P(), P(), P("px", "py"))
    out_specs = (P(None, "px", "py", None), P(), P(), P())
    return jax.shard_map(body, mesh=mesh, in_specs=in_specs, out_specs=out_specs, check_vma=False)
```

```python
import jax
import jax.numpy as jnp
import numpy as np
from jax import lax
from jax.experimental import pallas as pl
from jax.experimental.pallas import tpu as pltpu
from jax.sharding import PartitionSpec as P

f32, bf16 = jnp.float32, jnp.bfloat16
AXES = ("px", "py")
LANES = 640
ROWS = 40
NT = (((1,), (1,)), ((), ()))


def selections():
    pick = np.zeros((512, 216), np.float32)
    pick_target = np.zeros((256, 96), np.float32)
    for y in range(16):
        for c in range(3):
            for ox in range(3):
                for oy in range(3):
                    pick[y * 32 + c * 9 + ox * 3 + oy, (c * 3 + ox) * 24 + y + oy + 3] = 1
        for c in range(6):
            pick_target[y * 16 + c, c * 16 + y] = 1
    order = np.zeros((81, 96), np.float32)
    for oz in range(3):
        for c in range(3):
            for o in range(9):
                order[c * 27 + o * 3 + oz, oz * 32 + c * 9 + o] = 1
    return pick, pick_target, order


def dot(a, b):
    return jnp.dot(a, b, preferred_element_type=f32)


def dot_cells(a, b):
    return lax.dot_general(a, b, NT, preferred_element_type=f32)


def shift_z(value):
    return pltpu.roll(value, LANES - 1, 1) - pltpu.roll(value, 1, 1)


def differences(field, plane, row):
    here = pl.ds(row, 8)
    center = [field[c, plane, here, :] for c in range(3)]
    along_x = [field[c, plane + 1, here, :] - field[c, plane - 1, here, :] for c in range(3)]
    along_y = [field[c, plane, pl.ds(row + 1, 8), :] - field[c, plane, pl.ds(row - 1, 8), :] for c in range(3)]
    along_z = [shift_z(center[c]) for c in range(3)]
    return center, (along_x, along_y, along_z)


def stress_rows(field, plane, tau, tau_plane, row):
    _, d = differences(field, plane, row)
    xy, xz, yz = d[0][1] + d[1][0], d[0][2] + d[2][0], d[1][2] + d[2][1]
    diagonal = d[0][0] * d[0][0] + d[1][1] * d[1][1] + d[2][2] * d[2][2]
    mixed = xy * xy + xz * xz + yz * yz
    nu = 0.05 + 0.04 * jnp.sqrt(0.5 * diagonal + 0.25 * mixed)
    half = -0.5 * nu
    rows = pl.ds(row, 8)
    for c in range(3):
        tau[c, tau_plane, rows, :] = -nu * d[c][c]
    tau[3, tau_plane, rows, :] = half * xy
    tau[4, tau_plane, rows, :] = half * xz
    tau[5, tau_plane, rows, :] = half * yz


def step_rows(field, plane, tau, tau_plane, row):
    center, d = differences(field, plane, row)
    here = pl.ds(row, 8)

    def tau_x(c):
        return tau[c, tau_plane + 1, here, :] - tau[c, tau_plane - 1, here, :]

    def tau_y(c):
        return tau[c, tau_plane, pl.ds(row + 1, 8), :] - tau[c, tau_plane, pl.ds(row - 1, 8), :]

    def tau_z(c):
        return shift_z(tau[c, tau_plane, here, :])

    parts = ((0, 3, 4), (3, 1, 5), (4, 5, 2))
    out = []
    for j in range(3):
        a, b, c = parts[j]
        total = tau_x(a) + tau_y(b) + tau_z(c)
        total += center[0] * d[0][j] + center[1] * d[1][j] + center[2] * d[2][j]
        new = center[j] - 0.05 * total
        out.append(new + 0.005 if j == 0 else new)
    return out


def add_columns(tile, tile_target, starts, weights, totals):
    w1, w2, w2t, w3, w3t = weights
    g1, g2, g3 = totals
    columns, targets = [], []
    for n, first in enumerate(starts):
        start = first + 127
        base_lane = pl.multiple_of(lax.shift_right_logical(start, 7) * 128, 128)
        turn = (512 - (start & 127)) & 511
        window = pltpu.roll(tile[n * 32 : n * 32 + 32, pl.ds(base_lane, 512)], turn, 1)
        columns.append(jnp.concatenate([window[:, 0:256], window[:, 1:257], window[:, 2:258]], 0))
        target = pltpu.roll(tile_target[n * 16 : n * 16 + 16, pl.ds(base_lane, 512)], turn, 1)
        targets.append(target[:, 1:257])
    cols = jnp.concatenate(columns, 1)
    target = jnp.concatenate(targets, 1)
    h1 = dot(w1[...], cols)
    t1 = jnp.tanh(h1)
    q1 = h1 * t1
    a1 = (h1 + q1).astype(bf16)
    s1 = (1.0 + t1) * (1.0 + (h1 - q1))
    h2 = dot(w2[...], a1)
    t2 = jnp.tanh(h2)
    q2 = h2 * t2
    a2 = (h2 + q2).astype(bf16)
    s2 = (1.0 + t2) * (1.0 + (h2 - q2))
    misfit = dot(w3[...], jnp.concatenate([a2, target], 0)).astype(bf16)
    b2 = (dot(w3t[...], misfit) * s2).astype(bf16)
    b1 = (dot(w2t[...], b2) * s1).astype(bf16)
    g3[...] += dot_cells(misfit, a2)
    g2[...] += dot_cells(b2, a1)
    g1[...] += dot_cells(b1, cols)


def input_rows(field, plane):
    rows = [field[c, plane + ox - 1, 8:32, 0:512] for c in range(3) for ox in range(3)]
    return jnp.concatenate(rows, 0).astype(bf16)


def target_rows(tau, plane):
    return jnp.concatenate([tau[c, plane, 12:28, 0:512].astype(bf16) for c in range(6)], 0)


def gather(tile, at, table, rows):
    tile[at : at + table.shape[0], 128:640] = dot(table, rows).astype(bf16)


def clear_edges(*tiles):
    for tile in tiles:
        edge = jnp.zeros((tile.shape[0], 128), bf16)
        tile[:, 0:128] = edge
        tile[:, 640:768] = edge


def clear_rest(field):
    beyond = jnp.zeros((ROWS, 128), f32)
    strip = jnp.zeros((8, LANES), f32)
    for c in range(3):
        for p in range(field.shape[1]):
            field[c, p, :, 512:640] = beyond
            field[c, p, 4:12, :] = strip
            field[c, p, 28:36, :] = strip


def interior_kernel(
    offs, own, first, mid, last, pick, pick_target, order,
    w1, w2, w2t, w3, w3t, g1, g2, g3, field, tau, tile, tile_target,
):
    rows, cols = lax.broadcasted_iota(jnp.int32, (64, 64), 0), lax.broadcasted_iota(jnp.int32, (64, 64), 1)
    half = jnp.where(rows == cols, 0.5, 0.0).astype(bf16)
    w1[...] = (0.5 * dot(first[...], order[...])).astype(bf16)
    w2[...] = (0.5 * mid[...].astype(f32)).astype(bf16)
    w2t[...] = dot_cells(half, mid[...]).astype(bf16)
    rows, cols = lax.broadcasted_iota(jnp.int32, (16, 16), 0), lax.broadcasted_iota(jnp.int32, (16, 16), 1)
    minus = jnp.where(rows == cols, -1.0, 0.0)
    last_rows = jnp.concatenate([last[...].astype(f32), jnp.zeros((10, 64), f32)], 0)
    w3[...] = jnp.concatenate([last_rows, minus], 1).astype(bf16)
    w3t[...] = dot_cells(half, last_rows.astype(bf16)).astype(bf16)
    for total in (g1, g2, g3):
        total[...] = jnp.zeros_like(total)
    clear_edges(tile, tile_target)
    clear_rest(field)
    for c in range(3):
        for p in range(4):
            field[c, p, 12:28, 0:512] = own[c, p]

    def step(n, _):
        x = n + 1
        for row in (12, 20):
            stress_rows(field, x, tau, n, row)
        gather(tile, 0, pick[...], input_rows(field, x))
        gather(tile_target, 0, pick_target[...], target_rows(tau, n))
        starts = [offs[x, y] for y in range(1, 15)]
        add_columns(tile.at[32:480], tile_target.at[16:240], starts, (w1, w2, w2t, w3, w3t), (g1, g2, g3))
        return 0

    lax.fori_loop(0, 2, step, 0)


def rim_kernel(
    offs, own, x_low, x_high, y_low, y_high, w1, w2, w2t, w3, w3t, h1, h2, h3, pick, pick_target,
    g1, g2, g3, field, tau, tile, tile_target,
):
    g1[...] = h1[...]
    g2[...] = h2[...]
    g3[...] = h3[...]
    clear_edges(tile, tile_target)
    clear_rest(field)
    for c in range(3):
        for p in range(6):
            source, q = (x_low, 0) if p == 0 else (x_high, 0) if p == 5 else (own, p - 1)
            field[c, p, 12:28, 0:512] = source[c, q]
            field[c, p, 11:12, 0:512] = y_low[c, p]
            field[c, p, 28:29, 0:512] = y_high[c, p]

    def stress(p, _):
        for row in (12, 20):
            stress_rows(field, p + 1, tau, p, row)
        return 0

    lax.fori_loop(0, 4, stress, 0)

    def step(n, _):
        x, inner = 3 * n, 1 + n
        gather(tile, 0, pick[...], input_rows(field, x + 1))
        gather(tile_target, 0, pick_target[...], target_rows(tau, x))
        rows = input_rows(field, inner + 1)
        gather(tile, 512, pick[0:32, :], rows)
        gather(tile, 544, pick[480:512, :], rows)
        rows = target_rows(tau, inner)
        gather(tile_target, 256, pick_target[0:16, :], rows)
        gather(tile_target, 272, pick_target[240:256, :], rows)
        starts = [offs[x, y] for y in range(16)] + [offs[inner, 0], offs[inner, 15]]
        add_columns(tile, tile_target, starts, (w1, w2, w2t, w3, w3t), (g1, g2, g3))
        return 0

    lax.fori_loop(0, 2, step, 0)


def middle_kernel(
    offs, own, x_low, x_high, y_low, y_high, far_x_low, far_x_high, far_y_low, far_y_high,
    w1, w2, w2t, w3, w3t, h1, h2, h3, pick, pick_target, order,
    middle, packed, field, tau, tile, tile_target, g1, g2, g3,
):
    g1[...] = h1[...]
    g2[...] = h2[...]
    g3[...] = h3[...]
    clear_edges(tile, tile_target)
    clear_rest(field)
    line = jnp.zeros((1, LANES), f32)
    for c in range(6):
        for p in range(10):
            tau[c, p, 7:8, :] = line
            tau[c, p, 32:33, :] = line
    for c in range(3):
        for p in range(12):
            if p < 3:
                center = far_x_low[c, p].astype(f32)
            elif p > 8:
                center = far_x_high[c, p - 8].astype(f32)
            else:
                source, q = (x_low, 0) if p == 3 else (x_high, 0) if p == 8 else (own, p - 4)
                center = source[c, q]
            field[c, p, 12:28, 0:512] = center
            field[c, p, 8:12, 0:512] = far_y_low[c, p].astype(f32)
            field[c, p, 28:32, 0:512] = far_y_high[c, p].astype(f32)
            if 3 <= p <= 8:
                field[c, p, 11:12, 0:512] = y_low[c, p - 3]
                field[c, p, 28:29, 0:512] = y_high[c, p - 3]

    def stress_zero(p, _):
        for row in (8, 16, 24):
            stress_rows(field, p + 1, tau, p, row)
        return 0

    lax.fori_loop(0, 10, stress_zero, 0)
    inside = lax.broadcasted_iota(jnp.int32, (8, LANES), 1) < 512

    def advance_middle(p, _):
        for row in (8, 16, 24):
            new = step_rows(field, p + 2, tau, p + 1, row)
            for c in range(3):
                middle[c, p, pl.ds(row, 8), :] = jnp.where(inside, new[c], 0.0)
        return 0

    lax.fori_loop(0, 8, advance_middle, 0)

    def step(x, _):
        for row in (12, 20):
            stress_rows(middle, x + 2, tau, 0, row)
        gather(tile, 0, pick[...], input_rows(middle, x + 2))
        gather(tile_target, 0, pick_target[...], target_rows(tau, 0))
        starts = [offs[x, y] for y in range(16)]
        add_columns(tile, tile_target, starts, (w1, w2, w2t, w3, w3t), (g1, g2, g3))
        return 0

    lax.fori_loop(0, 4, step, 0)
    scale = 0.5**22
    ordered = lax.dot_general(
        g1[...], order[...].astype(f32), NT, preferred_element_type=f32, precision=lax.Precision.HIGHEST
    )
    mids = g2[...]
    packed[0:64, :] = scale * jnp.concatenate([ordered, jnp.zeros((64, 15), f32), mids[:, 0:32]], 1)
    packed[64:80, :] = scale * jnp.concatenate([mids[16 * k : 16 * k + 16, 32:64] for k in range(4)], 1)
    packed[80:88, :] = scale * jnp.concatenate([g3[0:8, :], jnp.zeros((8, 64), f32)], 1)


def final_kernel(middle, final, tau):
    def stress_one(p, _):
        for row in (8, 16, 24):
            stress_rows(middle, p + 1, tau, p, row)
        return 0

    lax.fori_loop(0, 6, stress_one, 0)

    def advance_final(p, _):
        for row in (12, 20):
            new = step_rows(middle, p + 2, tau, p + 1, row)
            for c in range(3):
                final[c, p, row - 12 : row - 4, :] = new[c][:, 0:512]
        return 0

    lax.fori_loop(0, 4, advance_final, 0)


def last_sum_kernel(a, b, c, d, first, mid, last):
    total = (a[...] + b[...]) + (c[...] + d[...])
    first[...] = total[0:64, 0:81]
    rest = jnp.concatenate([total[64:80, 32 * k : 32 * k + 32] for k in range(4)], 0)
    mid[...] = jnp.concatenate([total[0:64, 96:128], rest], 1)
    last[...] = total[80:86, 0:64]


def shaped(*dims, kind=f32):
    return jax.ShapeDtypeStruct(dims, kind)


WEIGHTS = [shaped(64, 96, kind=bf16), shaped(64, 64, kind=bf16), shaped(64, 64, kind=bf16),
           shaped(16, 80, kind=bf16), shaped(64, 16, kind=bf16)]
TOTALS = [shaped(64, 96), shaped(64, 64), shaped(16, 64)]


def call(kernel, args, out_shape, scratch, smem=0):
    vmem = pl.BlockSpec(memory_space=pltpu.VMEM)
    scalar = pl.BlockSpec(memory_space=pltpu.SMEM)
    return pl.pallas_call(
        kernel,
        in_specs=[scalar] * smem + [vmem] * (len(args) - smem),
        out_specs=[vmem] * len(out_shape),
        out_shape=out_shape,
        scratch_shapes=scratch,
        compiler_params=pltpu.CompilerParams(vmem_limit_bytes=48 * 2**20),
    )(*args)


def columns_scratch(planes, stress_planes, columns):
    return [
        pltpu.VMEM((3, planes, ROWS, LANES), f32),
        pltpu.VMEM((6, stress_planes, ROWS, LANES), f32),
        pltpu.VMEM((32 * columns, 768), bf16),
        pltpu.VMEM((16 * columns, 768), bf16),
    ]


def pairs(move):
    return [(i * 16 + j, (move(i, j)[0] % 8) * 16 + move(i, j)[1] % 16) for i in range(8) for j in range(16)]


ROTATIONS = (lambda k: (k + 1) % 4, lambda k: (k - 1) % 4, lambda k: (k + 2) % 4)


def along_y(turn):
    return lambda i, j: (i & 4 | turn(i & 3), j)


def along_x(turn):
    return lambda i, j: (i, j & 9 | turn(j >> 1 & 3) << 1)


def along_z(turn):
    def move(i, j):
        z = turn((j >> 3) * 2 + (i >> 2))
        return ((z & 1) * 4 + (i & 3), (z >> 1) * 8 + (j & 7))

    return move


def send(value, move):
    return lax.ppermute(value, AXES, pairs(move))


def body(velocity, first_weight, mid_weight, last_weight, offsets):
    pick, pick_target, order = (jnp.asarray(table, bf16) for table in selections())
    up, down = lambda i, j: (i + 1, j), lambda i, j: (i - 1, j)
    right, left = lambda i, j: (i, j + 1), lambda i, j: (i, j - 1)
    x_low = send(velocity[:, 3:4], up)
    x_high = send(velocity[:, 0:1], down)
    coarse = velocity.astype(bf16)
    far_x_low = send(coarse, up)
    far_x_high = send(coarse, down)

    *weights, h1, h2, h3 = call(
        interior_kernel,
        (offsets, velocity, first_weight, mid_weight, last_weight, pick, pick_target, order),
        WEIGHTS + TOTALS, columns_scratch(4, 2, 16), 1,
    )

    near = jnp.concatenate([x_low, velocity, x_high], 1)
    y_low = send(near[:, :, 15:16, :], right)
    y_high = send(near[:, :, 0:1, :], left)
    wide = jnp.concatenate([far_x_low, coarse, far_x_high], 1)
    far_y_low = send(wide[:, :, 12:16, :], right)
    far_y_high = send(wide[:, :, 0:4, :], left)

    totals = call(
        rim_kernel,
        (offsets, velocity, x_low, x_high, y_low, y_high, *weights, h1, h2, h3, pick, pick_target),
        TOTALS, columns_scratch(6, 4, 18), 1,
    )
    middle, packed = call(
        middle_kernel,
        (offsets, velocity, x_low, x_high, y_low, y_high, far_x_low, far_x_high, far_y_low, far_y_high,
         *weights, *totals, pick, pick_target, order),
        [shaped(3, 8, ROWS, LANES), shaped(88, 128)],
        columns_scratch(12, 10, 16) + [pltpu.VMEM(t.shape, f32) for t in TOTALS], 1,
    )
    (final,) = call(final_kernel, (middle,), [shaped(3, 4, 16, 512)], [pltpu.VMEM((6, 6, ROWS, LANES), f32)])

    packed = packed + send(packed, lambda i, j: (i, j ^ 1))
    for along in (along_y, along_x):
        a, b, c = (send(packed, along(turn)) for turn in ROTATIONS)
        packed = (packed + a) + (b + c)
    a, b, c = (send(packed, along_z(turn)) for turn in ROTATIONS)
    grads = call(last_sum_kernel, (packed, a, b, c), [shaped(64, 81), shaped(64, 64), shaped(6, 64)], [])
    return final, *grads


def solution(mesh):
    in_specs = (P(None, "px", "py", None), P(), P(), P(), P("px", "py"))
    out_specs = (P(None, "px", "py", None), P(), P(), P())
    return jax.shard_map(body, mesh=mesh, in_specs=in_specs, out_specs=out_specs, check_vma=False)
```

```python
import jax
import jax.numpy as jnp
import numpy as np
from jax import lax
from jax.experimental import pallas as pl
from jax.experimental.pallas import tpu as pltpu
from jax.sharding import PartitionSpec as P

f32, bf16 = jnp.float32, jnp.bfloat16
AXES = ("px", "py")
LANES = 640
ROWS = 40
NT = (((1,), (1,)), ((), ()))


def selections():
    pick = np.zeros((512, 216), np.float32)
    pick_target = np.zeros((256, 96), np.float32)
    for y in range(16):
        for c in range(3):
            for ox in range(3):
                for oy in range(3):
                    pick[y * 32 + c * 9 + ox * 3 + oy, (c * 3 + ox) * 24 + y + oy + 3] = 1
        for c in range(6):
            pick_target[y * 16 + c, c * 16 + y] = 1
    order = np.zeros((81, 96), np.float32)
    for oz in range(3):
        for c in range(3):
            for o in range(9):
                order[c * 27 + o * 3 + oz, oz * 32 + c * 9 + o] = 1
    return pick, pick_target, order


def dot(a, b):
    return jnp.dot(a, b, preferred_element_type=f32)


def dot_cells(a, b):
    return lax.dot_general(a, b, NT, preferred_element_type=f32)


def shift_z(value):
    return pltpu.roll(value, LANES - 1, 1) - pltpu.roll(value, 1, 1)


def differences(field, plane, row):
    here = pl.ds(row, 8)
    center = [field[c, plane, here, :] for c in range(3)]
    along_x = [field[c, plane + 1, here, :] - field[c, plane - 1, here, :] for c in range(3)]
    along_y = [field[c, plane, pl.ds(row + 1, 8), :] - field[c, plane, pl.ds(row - 1, 8), :] for c in range(3)]
    along_z = [shift_z(center[c]) for c in range(3)]
    return center, (along_x, along_y, along_z)


def stress_rows(field, plane, tau, tau_plane, row):
    _, d = differences(field, plane, row)
    xy, xz, yz = d[0][1] + d[1][0], d[0][2] + d[2][0], d[1][2] + d[2][1]
    diagonal = d[0][0] * d[0][0] + d[1][1] * d[1][1] + d[2][2] * d[2][2]
    mixed = xy * xy + xz * xz + yz * yz
    nu = 0.05 + 0.04 * jnp.sqrt(0.5 * diagonal + 0.25 * mixed)
    half = -0.5 * nu
    rows = pl.ds(row, 8)
    for c in range(3):
        tau[c, tau_plane, rows, :] = -nu * d[c][c]
    tau[3, tau_plane, rows, :] = half * xy
    tau[4, tau_plane, rows, :] = half * xz
    tau[5, tau_plane, rows, :] = half * yz


def step_rows(field, plane, tau, tau_plane, row):
    center, d = differences(field, plane, row)
    here = pl.ds(row, 8)

    def tau_x(c):
        return tau[c, tau_plane + 1, here, :] - tau[c, tau_plane - 1, here, :]

    def tau_y(c):
        return tau[c, tau_plane, pl.ds(row + 1, 8), :] - tau[c, tau_plane, pl.ds(row - 1, 8), :]

    def tau_z(c):
        return shift_z(tau[c, tau_plane, here, :])

    parts = ((0, 3, 4), (3, 1, 5), (4, 5, 2))
    out = []
    for j in range(3):
        a, b, c = parts[j]
        total = tau_x(a) + tau_y(b) + tau_z(c)
        total += center[0] * d[0][j] + center[1] * d[1][j] + center[2] * d[2][j]
        new = center[j] - 0.05 * total
        out.append(new + 0.005 if j == 0 else new)
    return out


def add_columns(tile, tile_target, starts, weights, totals):
    w1, w2, w2t, w3, w3t = weights
    g1, g2, g3 = totals
    columns, targets = [], []
    for n, first in enumerate(starts):
        start = first + 127
        base_lane = pl.multiple_of(lax.shift_right_logical(start, 7) * 128, 128)
        turn = (512 - (start & 127)) & 511
        window = pltpu.roll(tile[n * 32 : n * 32 + 32, pl.ds(base_lane, 512)], turn, 1)
        columns.append(jnp.concatenate([window[:, 0:256], window[:, 1:257], window[:, 2:258]], 0))
        target = pltpu.roll(tile_target[n * 16 : n * 16 + 16, pl.ds(base_lane, 512)], turn, 1)
        targets.append(target[:, 1:257])
    cols = jnp.concatenate(columns, 1)
    target = jnp.concatenate(targets, 1)
    h1 = dot(w1[...], cols)
    t1 = jnp.tanh(h1)
    q1 = h1 * t1
    a1 = (h1 + q1).astype(bf16)
    s1 = (1.0 + t1) * (1.0 + (h1 - q1))
    h2 = dot(w2[...], a1)
    t2 = jnp.tanh(h2)
    q2 = h2 * t2
    a2 = (h2 + q2).astype(bf16)
    s2 = (1.0 + t2) * (1.0 + (h2 - q2))
    misfit = dot(w3[...], jnp.concatenate([a2, target], 0)).astype(bf16)
    b2 = (dot(w3t[...], misfit) * s2).astype(bf16)
    b1 = (dot(w2t[...], b2) * s1).astype(bf16)
    g3[...] += dot_cells(misfit, a2)
    g2[...] += dot_cells(b2, a1)
    g1[...] += dot_cells(b1, cols)


def input_rows(field, plane):
    rows = [field[c, plane + ox - 1, 8:32, 0:512] for c in range(3) for ox in range(3)]
    return jnp.concatenate(rows, 0).astype(bf16)


def target_rows(tau, plane):
    return jnp.concatenate([tau[c, plane, 12:28, 0:512].astype(bf16) for c in range(6)], 0)


def gather(tile, at, table, rows):
    tile[at : at + table.shape[0], 128:640] = dot(table, rows).astype(bf16)


def clear_edges(*tiles):
    for tile in tiles:
        edge = jnp.zeros((tile.shape[0], 128), bf16)
        tile[:, 0:128] = edge
        tile[:, 640:768] = edge


def clear_rest(field):
    beyond = jnp.zeros((ROWS, 128), f32)
    strip = jnp.zeros((8, LANES), f32)
    for c in range(3):
        for p in range(field.shape[1]):
            field[c, p, :, 512:640] = beyond
            field[c, p, 4:12, :] = strip
            field[c, p, 28:36, :] = strip


def interior_kernel(
    offs, own, first, mid, last, pick, pick_target, order,
    w1, w2, w2t, w3, w3t, g1, g2, g3, field, tau, tile, tile_target,
):
    rows, cols = lax.broadcasted_iota(jnp.int32, (64, 64), 0), lax.broadcasted_iota(jnp.int32, (64, 64), 1)
    half = jnp.where(rows == cols, 0.5, 0.0).astype(bf16)
    w1[...] = (0.5 * dot(first[...], order[...])).astype(bf16)
    w2[...] = (0.5 * mid[...].astype(f32)).astype(bf16)
    w2t[...] = dot_cells(half, mid[...]).astype(bf16)
    rows, cols = lax.broadcasted_iota(jnp.int32, (16, 16), 0), lax.broadcasted_iota(jnp.int32, (16, 16), 1)
    minus = jnp.where(rows == cols, -1.0, 0.0)
    last_rows = jnp.concatenate([last[...].astype(f32), jnp.zeros((10, 64), f32)], 0)
    w3[...] = jnp.concatenate([last_rows, minus], 1).astype(bf16)
    w3t[...] = dot_cells(half, last_rows.astype(bf16)).astype(bf16)
    for total in (g1, g2, g3):
        total[...] = jnp.zeros_like(total)
    clear_edges(tile, tile_target)
    clear_rest(field)
    for c in range(3):
        for p in range(4):
            field[c, p, 12:28, 0:512] = own[c, p]

    def step(n, _):
        x = n + 1
        for row in (12, 20):
            stress_rows(field, x, tau, n, row)
        gather(tile, 0, pick[...], input_rows(field, x))
        gather(tile_target, 0, pick_target[...], target_rows(tau, n))
        starts = [offs[x, y] for y in range(1, 15)]
        add_columns(tile.at[32:480], tile_target.at[16:240], starts, (w1, w2, w2t, w3, w3t), (g1, g2, g3))
        return 0

    lax.fori_loop(0, 2, step, 0)


def side_kernel(
    offs, own, x_low, x_high, w1, w2, w2t, w3, w3t, h1, h2, h3, pick, pick_target,
    g1, g2, g3, field, tau, tile, tile_target,
):
    g1[...] = h1[...]
    g2[...] = h2[...]
    g3[...] = h3[...]
    clear_edges(tile, tile_target)
    clear_rest(field)
    for c in range(3):
        for p in range(6):
            source, q = (x_low, 3) if p == 0 else (x_high, 0) if p == 5 else (own, p - 1)
            field[c, p, 12:28, 0:512] = source[c, q]

    def step(n, _):
        x = 3 * n
        for row in (12, 20):
            stress_rows(field, x + 1, tau, 0, row)
        gather(tile, 0, pick[...], input_rows(field, x + 1))
        gather(tile_target, 0, pick_target[...], target_rows(tau, 0))
        starts = [offs[x, y] for y in range(1, 15)]
        add_columns(tile.at[32:480], tile_target.at[16:240], starts, (w1, w2, w2t, w3, w3t), (g1, g2, g3))
        return 0

    lax.fori_loop(0, 2, step, 0)


def middle_kernel(
    offs, own, x_low, x_high, y_low, y_high,
    w1, w2, w2t, w3, w3t, h1, h2, h3, pick, pick_target, order,
    middle, packed, field, tau, tile, tile_target, g1, g2, g3,
):
    g1[...] = h1[...]
    g2[...] = h2[...]
    g3[...] = h3[...]
    clear_edges(tile, tile_target)
    clear_rest(field)
    line = jnp.zeros((1, LANES), f32)
    for c in range(6):
        for p in range(10):
            tau[c, p, 7:8, :] = line
            tau[c, p, 32:33, :] = line
    for c in range(3):
        for p in range(12):
            source, q = ((x_low, p), (own, p - 4), (x_high, p - 8))[p // 4]
            field[c, p, 12:28, 0:512] = source[c, q]
            field[c, p, 8:12, 0:512] = y_low[c, p]
            field[c, p, 28:32, 0:512] = y_high[c, p]

    def stress_zero(p, _):
        for row in (8, 16, 24):
            stress_rows(field, p + 1, tau, p, row)
        return 0

    lax.fori_loop(0, 10, stress_zero, 0)
    inside = lax.broadcasted_iota(jnp.int32, (8, LANES), 1) < 512

    def advance_middle(p, _):
        for row in (8, 16, 24):
            new = step_rows(field, p + 2, tau, p + 1, row)
            for c in range(3):
                middle[c, p, pl.ds(row, 8), :] = jnp.where(inside, new[c], 0.0)
        return 0

    lax.fori_loop(0, 8, advance_middle, 0)

    def step(x, _):
        rows = input_rows(field, x + 4)
        gather(tile, 512, pick[0:32, :], rows)
        gather(tile, 544, pick[480:512, :], rows)
        rows = target_rows(tau, x + 3)
        gather(tile_target, 256, pick_target[0:16, :], rows)
        gather(tile_target, 272, pick_target[240:256, :], rows)
        for row in (12, 20):
            stress_rows(middle, x + 2, tau, 0, row)
        gather(tile, 0, pick[...], input_rows(middle, x + 2))
        gather(tile_target, 0, pick_target[...], target_rows(tau, 0))
        starts = [offs[x, y] for y in range(16)] + [offs[x, 0], offs[x, 15]]
        add_columns(tile, tile_target, starts, (w1, w2, w2t, w3, w3t), (g1, g2, g3))
        return 0

    lax.fori_loop(0, 4, step, 0)
    scale = 0.5**22
    ordered = lax.dot_general(
        g1[...], order[...].astype(f32), NT, preferred_element_type=f32, precision=lax.Precision.HIGHEST
    )
    mids = g2[...]
    packed[0:64, :] = scale * jnp.concatenate([ordered, jnp.zeros((64, 15), f32), mids[:, 0:32]], 1)
    packed[64:80, :] = scale * jnp.concatenate([mids[16 * k : 16 * k + 16, 32:64] for k in range(4)], 1)
    packed[80:88, :] = scale * jnp.concatenate([g3[0:8, :], jnp.zeros((8, 64), f32)], 1)


def final_kernel(middle, final, tau):
    def stress_one(p, _):
        for row in (8, 16, 24):
            stress_rows(middle, p + 1, tau, p, row)
        return 0

    lax.fori_loop(0, 6, stress_one, 0)

    def advance_final(p, _):
        for row in (12, 20):
            new = step_rows(middle, p + 2, tau, p + 1, row)
            for c in range(3):
                final[c, p, row - 12 : row - 4, :] = new[c][:, 0:512]
        return 0

    lax.fori_loop(0, 4, advance_final, 0)


def last_sum_kernel(a, b, c, d, first, mid, last):
    total = (a[...] + b[...]) + (c[...] + d[...])
    first[...] = total[0:64, 0:81]
    rest = jnp.concatenate([total[64:80, 32 * k : 32 * k + 32] for k in range(4)], 0)
    mid[...] = jnp.concatenate([total[0:64, 96:128], rest], 1)
    last[...] = total[80:86, 0:64]


def shaped(*dims, kind=f32):
    return jax.ShapeDtypeStruct(dims, kind)


WEIGHTS = [shaped(64, 96, kind=bf16), shaped(64, 64, kind=bf16), shaped(64, 64, kind=bf16),
           shaped(16, 80, kind=bf16), shaped(64, 16, kind=bf16)]
TOTALS = [shaped(64, 96), shaped(64, 64), shaped(16, 64)]


def call(kernel, args, out_shape, scratch, smem=0, us=1, mib=48):
    vmem = pl.BlockSpec(memory_space=pltpu.VMEM)
    scalar = pl.BlockSpec(memory_space=pltpu.SMEM)
    return pl.pallas_call(
        kernel,
        in_specs=[scalar] * smem + [vmem] * (len(args) - smem),
        out_specs=[vmem] * len(out_shape),
        out_shape=out_shape,
        scratch_shapes=scratch,
        compiler_params=pltpu.CompilerParams(vmem_limit_bytes=mib * 2**20),
        cost_estimate=pl.CostEstimate(flops=int(us * 1.15e9), bytes_accessed=int(us * 3.69e6), transcendentals=0),
    )(*args)


def columns_scratch(planes, stress_planes, columns):
    return [
        pltpu.VMEM((3, planes, ROWS, LANES), f32),
        pltpu.VMEM((6, stress_planes, ROWS, LANES), f32),
        pltpu.VMEM((32 * columns, 768), bf16),
        pltpu.VMEM((16 * columns, 768), bf16),
    ]


def pairs(move):
    return [(i * 16 + j, (move(i, j)[0] % 8) * 16 + move(i, j)[1] % 16) for i in range(8) for j in range(16)]


EXCHANGES = (lambda k: k ^ 1, lambda k: k ^ 3, lambda k: k ^ 2)


def along_y(turn):
    return lambda i, j: (i & 4 | turn(i & 3), j)


def along_x(turn):
    return lambda i, j: (i, j & 9 | turn(j >> 1 & 3) << 1)


def along_z(turn):
    def move(i, j):
        z = turn((j >> 3) * 2 + (i >> 2))
        return ((z & 1) * 4 + (i & 3), (z >> 1) * 8 + (j & 7))

    return move


def send(value, move):
    return lax.ppermute(value, AXES, pairs(move))


def body(velocity, first_weight, mid_weight, last_weight, offsets):
    pick, pick_target, order = (jnp.asarray(table, bf16) for table in selections())
    up, down = lambda i, j: (i + 1, j), lambda i, j: (i - 1, j)
    right, left = lambda i, j: (i, j + 1), lambda i, j: (i, j - 1)
    x_low, x_high = send(velocity, up), send(velocity, down)
    *weights, h1, h2, h3 = call(
        interior_kernel,
        (offsets, velocity, first_weight, mid_weight, last_weight, pick, pick_target, order),
        WEIGHTS + TOTALS, columns_scratch(4, 2, 16), 1, 6, 62,
    )
    x_low, x_high, h1 = lax.optimization_barrier((x_low, x_high, h1))
    wide = jnp.concatenate([x_low, velocity, x_high], 1)
    y_low, y_high = send(wide[:, :, 12:16, :], right), send(wide[:, :, 0:4, :], left)
    totals = call(
        side_kernel,
        (offsets, velocity, x_low, x_high, *weights, h1, h2, h3, pick, pick_target),
        TOTALS, columns_scratch(6, 1, 16), 1, 6,
    )
    middle, packed = call(
        middle_kernel,
        (offsets, velocity, x_low, x_high, y_low, y_high, *weights, *totals, pick, pick_target, order),
        [shaped(3, 8, ROWS, LANES), shaped(88, 128)],
        columns_scratch(12, 10, 18) + [pltpu.VMEM(t.shape, f32) for t in TOTALS], 1, 16,
    )
    (final,) = call(final_kernel, (middle,), [shaped(3, 4, 16, 512)], [pltpu.VMEM((6, 6, ROWS, LANES), f32)], 0, 3)

    packed = packed + send(packed, lambda i, j: (i, j ^ 1))
    for along in (along_y, along_x):
        a, b, c = (send(packed, along(turn)) for turn in EXCHANGES)
        packed = (packed + a) + (b + c)
    a, b, c = (send(packed, along_z(turn)) for turn in EXCHANGES)
    grads = call(last_sum_kernel, (packed, a, b, c), [shaped(64, 81), shaped(64, 64), shaped(6, 64)], [])
    return final, *grads


def solution(mesh):
    in_specs = (P(None, "px", "py", None), P(), P(), P(), P("px", "py"))
    out_specs = (P(None, "px", "py", None), P(), P(), P())
    return jax.shard_map(body, mesh=mesh, in_specs=in_specs, out_specs=out_specs, check_vma=False)
```

```python
import jax
import jax.numpy as jnp
import numpy as np
from jax import lax
from jax.experimental import pallas as pl
from jax.experimental.pallas import tpu as pltpu
from jax.sharding import PartitionSpec as P

f32, bf16 = jnp.float32, jnp.bfloat16
AXES = ("px", "py")
LANES = 640
ROWS = 40
NT = (((1,), (1,)), ((), ()))


def selections():
    table = np.zeros((864, 216), np.float32)
    for y in range(16):
        for c in range(3):
            for ox in range(3):
                for oy in range(3):
                    table[y * 32 + c * 9 + ox * 3 + oy, (c * 3 + ox) * 24 + y + oy + 3] = 1
        for c in range(6):
            table[512 + y * 16 + c, c * 16 + y] = 1
    for oz in range(3):
        for c in range(3):
            for o in range(9):
                table[768 + c * 27 + o * 3 + oz, oz * 32 + c * 9 + o] = 1
    return table


class Part:
    def __init__(self, ref, first, last, lanes):
        self.ref, self.first, self.last, self.lanes = ref, first, last, lanes

    def rows(self, first, last):
        return self.ref[self.first + first : self.first + last, 0 : self.lanes]

    def __getitem__(self, _):
        return self.ref[self.first : self.last, 0 : self.lanes]

    def __setitem__(self, _, value):
        self.ref[self.first : self.last, 0 : self.lanes] = value


def table_parts(table):
    return Part(table, 0, 512, 216), Part(table, 512, 768, 96), Part(table, 768, 849, 96)


def weight_parts(packed):
    return (Part(packed, 0, 64, 96), Part(packed, 64, 128, 64), Part(packed, 128, 192, 64),
            Part(packed, 192, 208, 80), Part(packed, 208, 272, 16))


def total_parts(packed):
    return Part(packed, 0, 64, 96), Part(packed, 64, 128, 64), Part(packed, 128, 144, 64)


def dot(a, b):
    return jnp.dot(a, b, preferred_element_type=f32)


def dot_cells(a, b):
    return lax.dot_general(a, b, NT, preferred_element_type=f32)


def shift_z(value):
    return pltpu.roll(value, LANES - 1, 1) - pltpu.roll(value, 1, 1)


def differences(field, plane, row):
    here = pl.ds(row, 8)
    center = [field[c, plane, here, :] for c in range(3)]
    along_x = [field[c, plane + 1, here, :] - field[c, plane - 1, here, :] for c in range(3)]
    along_y = [field[c, plane, pl.ds(row + 1, 8), :] - field[c, plane, pl.ds(row - 1, 8), :] for c in range(3)]
    along_z = [shift_z(center[c]) for c in range(3)]
    return center, (along_x, along_y, along_z)


def stress_rows(field, plane, tau, tau_plane, row):
    _, d = differences(field, plane, row)
    xy, xz, yz = d[0][1] + d[1][0], d[0][2] + d[2][0], d[1][2] + d[2][1]
    diagonal = d[0][0] * d[0][0] + d[1][1] * d[1][1] + d[2][2] * d[2][2]
    mixed = xy * xy + xz * xz + yz * yz
    nu = 0.05 + 0.04 * jnp.sqrt(0.5 * diagonal + 0.25 * mixed)
    half = -0.5 * nu
    rows = pl.ds(row, 8)
    for c in range(3):
        tau[c, tau_plane, rows, :] = -nu * d[c][c]
    tau[3, tau_plane, rows, :] = half * xy
    tau[4, tau_plane, rows, :] = half * xz
    tau[5, tau_plane, rows, :] = half * yz


def step_rows(field, plane, tau, tau_plane, row):
    center, d = differences(field, plane, row)
    here = pl.ds(row, 8)

    def tau_x(c):
        return tau[c, tau_plane + 1, here, :] - tau[c, tau_plane - 1, here, :]

    def tau_y(c):
        return tau[c, tau_plane, pl.ds(row + 1, 8), :] - tau[c, tau_plane, pl.ds(row - 1, 8), :]

    def tau_z(c):
        return shift_z(tau[c, tau_plane, here, :])

    parts = ((0, 3, 4), (3, 1, 5), (4, 5, 2))
    out = []
    for j in range(3):
        a, b, c = parts[j]
        total = tau_x(a) + tau_y(b) + tau_z(c)
        total += center[0] * d[0][j] + center[1] * d[1][j] + center[2] * d[2][j]
        new = center[j] - 0.05 * total
        out.append(new + 0.005 if j == 0 else new)
    return out


def add_columns(tile, tile_target, starts, weights, totals):
    w1, w2, w2t, w3, w3t = weights
    g1, g2, g3 = totals
    columns, targets = [], []
    for n, first in enumerate(starts):
        start = first + 127
        base_lane = pl.multiple_of(lax.shift_right_logical(start, 7) * 128, 128)
        turn = (512 - (start & 127)) & 511
        window = pltpu.roll(tile[n * 32 : n * 32 + 32, pl.ds(base_lane, 512)], turn, 1)
        columns.append(jnp.concatenate([window[:, 0:256], window[:, 1:257], window[:, 2:258]], 0))
        target = pltpu.roll(tile_target[n * 16 : n * 16 + 16, pl.ds(base_lane, 512)], turn, 1)
        targets.append(target[:, 1:257])
    cols = jnp.concatenate(columns, 1)
    target = jnp.concatenate(targets, 1)
    h1 = dot(w1[...], cols)
    t1 = jnp.tanh(h1)
    q1 = h1 * t1
    a1 = (h1 + q1).astype(bf16)
    s1 = (1.0 + t1) * (1.0 + (h1 - q1))
    h2 = dot(w2[...], a1)
    t2 = jnp.tanh(h2)
    q2 = h2 * t2
    a2 = (h2 + q2).astype(bf16)
    s2 = (1.0 + t2) * (1.0 + (h2 - q2))
    misfit = dot(w3[...], jnp.concatenate([a2, target], 0)).astype(bf16)
    b2 = (dot(w3t[...], misfit) * s2).astype(bf16)
    b1 = (dot(w2t[...], b2) * s1).astype(bf16)
    g3[...] += dot_cells(misfit, a2)
    g2[...] += dot_cells(b2, a1)
    g1[...] += dot_cells(b1, cols)


def input_rows(field, plane):
    rows = [field[c, plane + ox - 1, 8:32, 0:512] for c in range(3) for ox in range(3)]
    return jnp.concatenate(rows, 0).astype(bf16)


def target_rows(tau, plane):
    return jnp.concatenate([tau[c, plane, 12:28, 0:512].astype(bf16) for c in range(6)], 0)


def gather(tile, at, table, rows):
    tile[at : at + table.shape[0], 128:640] = dot(table, rows).astype(bf16)


def clear_edges(*tiles):
    for tile in tiles:
        edge = jnp.zeros((tile.shape[0], 128), bf16)
        tile[:, 0:128] = edge
        tile[:, 640:768] = edge


def clear_rest(field):
    beyond = jnp.zeros((ROWS, 128), f32)
    strip = jnp.zeros((8, LANES), f32)
    for c in range(3):
        for p in range(field.shape[1]):
            field[c, p, :, 512:640] = beyond
            field[c, p, 4:12, :] = strip
            field[c, p, 28:36, :] = strip


def interior_kernel(
    offs, own, first, mid, last, table, packed_weights, packed_totals, field, tau, tile, tile_target,
    local_table, local_first, local_mid, local_last, sems,
):
    pairs_in = ((first, local_first), (mid, local_mid), (last, local_last), (table, local_table))
    copies = [pltpu.make_async_copy(a, b, sems.at[k]) for k, (a, b) in enumerate(pairs_in)]
    for copy in copies:
        copy.start()
    clear_edges(tile, tile_target)
    clear_rest(field)
    for c in range(3):
        for p in range(4):
            field[c, p, 12:28, 0:512] = own[c, p]
    for copy in copies:
        copy.wait()
    first, mid, last = local_first, local_mid, local_last
    pick, pick_target, order = table_parts(local_table)
    weights, totals = weight_parts(packed_weights), total_parts(packed_totals)
    w1, w2, w2t, w3, w3t = weights
    rows, cols = lax.broadcasted_iota(jnp.int32, (64, 64), 0), lax.broadcasted_iota(jnp.int32, (64, 64), 1)
    half = jnp.where(rows == cols, 0.5, 0.0).astype(bf16)
    w1[...] = (0.5 * dot(first[...], order[...])).astype(bf16)
    w2[...] = (0.5 * mid[...].astype(f32)).astype(bf16)
    w2t[...] = dot_cells(half, mid[...]).astype(bf16)
    rows, cols = lax.broadcasted_iota(jnp.int32, (16, 16), 0), lax.broadcasted_iota(jnp.int32, (16, 16), 1)
    minus = jnp.where(rows == cols, -1.0, 0.0)
    last_rows = jnp.concatenate([last[...].astype(f32), jnp.zeros((10, 64), f32)], 0)
    w3[...] = jnp.concatenate([last_rows, minus], 1).astype(bf16)
    w3t[...] = dot_cells(half, last_rows.astype(bf16)).astype(bf16)
    packed_totals[...] = jnp.zeros_like(packed_totals)

    def step(n, _):
        x = n + 1
        for row in (12, 20):
            stress_rows(field, x, tau, n, row)
        gather(tile, 0, pick[...], input_rows(field, x))
        gather(tile_target, 0, pick_target[...], target_rows(tau, n))
        starts = [offs[x, y] for y in range(1, 15)]
        add_columns(tile.at[32:480], tile_target.at[16:240], starts, weights, totals)
        return 0

    lax.fori_loop(0, 2, step, 0)


def split_bf16(value):
    high = value.astype(bf16)
    return high, (value - high.astype(f32)).astype(bf16)


def pack_x_kernel(own, up, down):
    for c in range(3):
        for x in range(4):
            high, rest = split_bf16(own[c, x])
            up[c, x] = high
            down[c, x + 1] = high
            if x == 3:
                up[c, 4] = rest
            if x == 0:
                down[c, 0] = rest


def pack_y_kernel(own, x_low, x_high, right, left):
    for c in range(3):
        for out, first, near in ((right, 12, 15), (left, 0, 0)):
            rests = []
            for p in range(12):
                if p < 4:
                    high = x_low[c, p].astype(f32)
                elif p < 8:
                    high, rest = split_bf16(own[c, p - 4])
                    high, rest = high.astype(f32), rest.astype(f32)
                else:
                    high = x_high[c, p - 7].astype(f32)
                if p == 3:
                    rest = x_low[c, 4].astype(f32)
                if p == 8:
                    rest = x_high[c, 0].astype(f32)
                out[c, p] = high[first : first + 4, :].astype(bf16)
                if 3 <= p <= 8:
                    rests.append(rest[near : near + 1, :])
            rests = jnp.concatenate(rests + [jnp.zeros((2, 512), f32)], 0)
            out[c, 12] = rests[0:4].astype(bf16)
            out[c, 13] = rests[4:8].astype(bf16)


def x_plane(x_low, own, x_high, c, p):
    if p < 4:
        plane = x_low[c, p].astype(f32)
        return plane + x_low[c, 4].astype(f32) if p == 3 else plane
    if p < 8:
        return own[c, p - 4]
    plane = x_high[c, p - 7].astype(f32)
    return plane + x_high[c, 0].astype(f32) if p == 8 else plane


def side_kernel(
    offs, own, x_low, x_high, packed_weights, before, table, packed_totals, field, tau, tile, tile_target,
    local_table, sems,
):
    copy = pltpu.make_async_copy(table, local_table, sems.at[0])
    copy.start()
    pick, pick_target, _ = table_parts(local_table)
    weights, totals = weight_parts(packed_weights), total_parts(packed_totals)
    packed_totals[...] = before[...]
    clear_edges(tile, tile_target)
    clear_rest(field)
    for c in range(3):
        for p in range(6):
            field[c, p, 12:28, 0:512] = x_plane(x_low, own, x_high, c, p + 3)
    copy.wait()

    def step(n, _):
        x = 3 * n
        for row in (12, 20):
            stress_rows(field, x + 1, tau, 0, row)
        gather(tile, 0, pick[...], input_rows(field, x + 1))
        gather(tile_target, 0, pick_target[...], target_rows(tau, 0))
        starts = [offs[x, y] for y in range(1, 15)]
        add_columns(tile.at[32:480], tile_target.at[16:240], starts, weights, totals)
        return 0

    lax.fori_loop(0, 2, step, 0)


def middle_kernel(
    offs, own, x_low, x_high, y_low, y_high,
    packed_weights, before, table, middle, packed, field, tau, tile, tile_target,
    local_table, sems, packed_totals,
):
    copy = pltpu.make_async_copy(table, local_table, sems.at[0])
    copy.start()
    pick, pick_target, order = table_parts(local_table)
    weights, totals = weight_parts(packed_weights), total_parts(packed_totals)
    packed_totals[...] = before[...]
    g1, g2, g3 = totals
    clear_edges(tile, tile_target)
    clear_rest(field)
    line = jnp.zeros((1, LANES), f32)
    for c in range(6):
        for p in range(10):
            tau[c, p, 7:8, :] = line
            tau[c, p, 32:33, :] = line
    for c in range(3):
        for p in range(12):
            field[c, p, 12:28, 0:512] = x_plane(x_low, own, x_high, c, p)
            low, high = y_low[c, p].astype(f32), y_high[c, p].astype(f32)
            field[c, p, 8:12, 0:512] = low
            field[c, p, 28:32, 0:512] = high
            if 3 <= p <= 8:
                k, r = 12 + (p - 3) // 4, (p - 3) % 4
                field[c, p, 11:12, 0:512] = low[3:4] + y_low[c, k].astype(f32)[r : r + 1]
                field[c, p, 28:29, 0:512] = high[0:1] + y_high[c, k].astype(f32)[r : r + 1]

    def stress_zero(p, _):
        for row in (8, 16, 24):
            stress_rows(field, p + 1, tau, p, row)
        return 0

    lax.fori_loop(0, 10, stress_zero, 0)
    inside = lax.broadcasted_iota(jnp.int32, (8, LANES), 1) < 512

    def advance_middle(p, _):
        for row in (8, 16, 24):
            new = step_rows(field, p + 2, tau, p + 1, row)
            for c in range(3):
                middle[c, p, pl.ds(row, 8), :] = jnp.where(inside, new[c], 0.0)
        return 0

    lax.fori_loop(0, 8, advance_middle, 0)
    copy.wait()

    def step(x, _):
        rows = input_rows(field, x + 4)
        gather(tile, 512, pick.rows(0, 32), rows)
        gather(tile, 544, pick.rows(480, 512), rows)
        rows = target_rows(tau, x + 3)
        gather(tile_target, 256, pick_target.rows(0, 16), rows)
        gather(tile_target, 272, pick_target.rows(240, 256), rows)
        for row in (12, 20):
            stress_rows(middle, x + 2, tau, 0, row)
        gather(tile, 0, pick[...], input_rows(middle, x + 2))
        gather(tile_target, 0, pick_target[...], target_rows(tau, 0))
        starts = [offs[x, y] for y in range(16)] + [offs[x, 0], offs[x, 15]]
        add_columns(tile, tile_target, starts, weights, totals)
        return 0

    lax.fori_loop(0, 4, step, 0)
    scale = 0.5**22
    ordered = lax.dot_general(
        g1[...], order[...].astype(f32), NT, preferred_element_type=f32, precision=lax.Precision.HIGHEST
    )
    mids = g2[...]
    packed[0:64, :] = scale * jnp.concatenate([ordered, jnp.zeros((64, 15), f32), mids[:, 0:32]], 1)
    packed[64:80, :] = scale * jnp.concatenate([mids[16 * k : 16 * k + 16, 32:64] for k in range(4)], 1)
    packed[80:88, :] = scale * jnp.concatenate([g3[...][0:8], jnp.zeros((8, 64), f32)], 1)


def final_kernel(middle, final, tau):
    def stress_one(p, _):
        for row in (8, 16, 24):
            stress_rows(middle, p + 1, tau, p, row)
        return 0

    lax.fori_loop(0, 6, stress_one, 0)

    def advance_final(p, _):
        for row in (12, 20):
            new = step_rows(middle, p + 2, tau, p + 1, row)
            for c in range(3):
                final[c, p, row - 12 : row - 4, :] = new[c][:, 0:512]
        return 0

    lax.fori_loop(0, 4, advance_final, 0)


def last_sum_kernel(a, b, c, d, first, mid, last):
    total = (a[...] + b[...]) + (c[...] + d[...])
    first[...] = total[0:64, 0:81]
    rest = jnp.concatenate([total[64:80, 32 * k : 32 * k + 32] for k in range(4)], 0)
    mid[...] = jnp.concatenate([total[0:64, 96:128], rest], 1)
    last[...] = total[80:86, 0:64]


def shaped(*dims, kind=f32):
    return jax.ShapeDtypeStruct(dims, kind)


WEIGHTS, TOTALS = shaped(272, 128, kind=bf16), shaped(144, 128)


def call(kernel, args, out_shape, scratch, smem=0, us=1, mib=16, hbm=0):
    vmem = pl.BlockSpec(memory_space=pltpu.VMEM)
    scalar = pl.BlockSpec(memory_space=pltpu.SMEM)
    far = pl.BlockSpec(memory_space=pltpu.HBM)
    return pl.pallas_call(
        kernel,
        in_specs=[scalar] * smem + [vmem] * (len(args) - smem - hbm) + [far] * hbm,
        out_specs=[vmem] * len(out_shape),
        out_shape=out_shape,
        scratch_shapes=scratch,
        compiler_params=pltpu.CompilerParams(vmem_limit_bytes=mib * 2**20),
        cost_estimate=pl.CostEstimate(flops=int(us * 1.15e9), bytes_accessed=int(us * 3.69e6), transcendentals=0),
    )(*args)


def columns_scratch(planes, stress_planes, columns):
    return [
        pltpu.VMEM((3, planes, ROWS, LANES), f32),
        pltpu.VMEM((6, stress_planes, ROWS, LANES), f32),
        pltpu.VMEM((32 * columns, 768), bf16),
        pltpu.VMEM((16 * columns, 768), bf16),
        pltpu.VMEM((864, 216), bf16),
    ]


def pairs(move):
    return [(i * 16 + j, (move(i, j)[0] % 8) * 16 + move(i, j)[1] % 16) for i in range(8) for j in range(16)]


EXCHANGES = (lambda k: k ^ 1, lambda k: k ^ 3, lambda k: k ^ 2)


def along_y(turn):
    return lambda i, j: (i & 4 | turn(i & 3), j)


def along_x(turn):
    return lambda i, j: (i, j & 9 | turn(j >> 1 & 3) << 1)


def along_z(turn):
    def move(i, j):
        z = turn((j >> 3) * 2 + (i >> 2))
        return ((z & 1) * 4 + (i & 3), (z >> 1) * 8 + (j & 7))

    return move


def send(value, move):
    return lax.ppermute(value, AXES, pairs(move))


def body(velocity, first_weight, mid_weight, last_weight, offsets):
    table = jnp.asarray(selections(), bf16)
    up, down = lambda i, j: (i + 1, j), lambda i, j: (i - 1, j)
    right, left = lambda i, j: (i, j + 1), lambda i, j: (i, j - 1)
    to_up, to_down = call(pack_x_kernel, (velocity,), [shaped(3, 5, 16, 512, kind=bf16)] * 2, [])
    x_low, x_high = send(to_up, up), send(to_down, down)
    weights, totals = call(
        interior_kernel,
        (offsets, velocity, first_weight, mid_weight, last_weight, table),
        [WEIGHTS, TOTALS], columns_scratch(4, 2, 16)
        + [pltpu.VMEM(n, bf16) for n in ((64, 81), (64, 64), (6, 64))] + [pltpu.SemaphoreType.DMA((4,))],
        1, 6, 16, 4,
    )
    x_low, x_high, totals = lax.optimization_barrier((x_low, x_high, totals))
    to_right, to_left = call(
        pack_y_kernel, (velocity, x_low, x_high), [shaped(3, 14, 4, 512, kind=bf16)] * 2, []
    )
    y_low, y_high = send(to_right, right), send(to_left, left)
    (totals,) = call(
        side_kernel,
        (offsets, velocity, x_low, x_high, weights, totals, table),
        [TOTALS], columns_scratch(6, 1, 16) + [pltpu.SemaphoreType.DMA((1,))], 1, 6, 16, 1,
    )
    middle, packed = call(
        middle_kernel,
        (offsets, velocity, x_low, x_high, y_low, y_high, weights, totals, table),
        [shaped(3, 8, ROWS, LANES), shaped(88, 128)],
        columns_scratch(12, 10, 18) + [pltpu.SemaphoreType.DMA((1,)), pltpu.VMEM(TOTALS.shape, f32)], 1, 16, 32, 1,
    )
    (final,) = call(final_kernel, (middle,), [shaped(3, 4, 16, 512)], [pltpu.VMEM((6, 6, ROWS, LANES), f32)], 0, 3)

    packed = packed + send(packed, lambda i, j: (i, j ^ 1))
    for along in (along_y, along_x):
        a, b, c = (send(packed, along(turn)) for turn in EXCHANGES)
        packed = (packed + a) + (b + c)
    a, b, c = (send(packed, along_z(turn)) for turn in EXCHANGES)
    grads = call(last_sum_kernel, (packed, a, b, c), [shaped(64, 81), shaped(64, 64), shaped(6, 64)], [])
    return final, *grads


def solution(mesh):
    in_specs = (P(None, "px", "py", None), P(), P(), P(), P("px", "py"))
    out_specs = (P(None, "px", "py", None), P(), P(), P())
    return jax.shard_map(body, mesh=mesh, in_specs=in_specs, out_specs=out_specs, check_vma=False)
```

```python
import jax
import jax.numpy as jnp
import numpy as np
from jax import lax
from jax.experimental import pallas as pl
from jax.experimental.pallas import tpu as pltpu
from jax.sharding import PartitionSpec as P

f32, bf16 = jnp.float32, jnp.bfloat16
AXES = ("px", "py")
LANES = 512
ROWS = 40
NT = (((1,), (1,)), ((), ()))


def selections():
    table = np.zeros((960, 216), np.float32)
    for y in range(16):
        for c in range(3):
            for ox in range(3):
                for oy in range(3):
                    table[y * 32 + c * 9 + ox * 3 + oy, (c * 3 + ox) * 24 + y + oy + 3] = 1
        for c in range(6):
            table[512 + y * 16 + c, c * 16 + y] = 1
    for oz in range(3):
        for c in range(3):
            for o in range(9):
                table[768 + c * 27 + o * 3 + oz, oz * 32 + c * 9 + o] = 1
    table[864:928] = table[np.r_[0:32, 480:512]]
    table[928:960] = table[np.r_[512:528, 752:768]]
    return table


class Part:
    def __init__(self, ref, first, last, lanes):
        self.ref, self.first, self.last, self.lanes = ref, first, last, lanes

    def __getitem__(self, _):
        return self.ref[self.first : self.last, 0 : self.lanes]

    def __setitem__(self, _, value):
        self.ref[self.first : self.last, 0 : self.lanes] = value


def table_parts(table):
    return Part(table, 0, 512, 216), Part(table, 512, 768, 96), Part(table, 768, 849, 96)


def edge_parts(table):
    return Part(table, 864, 928, 216), Part(table, 928, 960, 96)


def weight_parts(packed):
    return (Part(packed, 0, 64, 96), Part(packed, 64, 192, 128), Part(packed, 192, 320, 128),
            Part(packed, 320, 352, 128), Part(packed, 352, 480, 32))


def total_parts(packed):
    return Part(packed, 0, 64, 96), Part(packed, 64, 128, 64), Part(packed, 128, 144, 64)


def dot(a, b):
    return jnp.dot(a, b, preferred_element_type=f32)


def dot_cells(a, b):
    return lax.dot_general(a, b, NT, preferred_element_type=f32)


def shift_z(value, below=0.0, above=0.0):
    up, down = pltpu.roll(value, LANES - 1, 1), pltpu.roll(value, 1, 1)
    lane = lax.broadcasted_iota(jnp.int32, (8, 128), 1)
    first = up[:, :128] - jnp.where(lane == 0, below, down[:, :128])
    last = jnp.where(lane == 127, above, up[:, 384:]) - down[:, 384:]
    return jnp.concatenate([first, up[:, 128:384] - down[:, 128:384], last], 1)


def wall_stress(velocity):
    x, y, z = velocity
    nu = 0.05 + 0.04 * jnp.sqrt(0.5 * z * z + 0.25 * (x * x + y * y))
    return {4: -0.5 * nu * x, 5: -0.5 * nu * y, 2: -nu * z}


def differences(field, plane, row):
    here = pl.ds(row, 8)
    center = [field[c, plane, here, :] for c in range(3)]
    along_x = [field[c, plane + 1, here, :] - field[c, plane - 1, here, :] for c in range(3)]
    along_y = [field[c, plane, pl.ds(row + 1, 8), :] - field[c, plane, pl.ds(row - 1, 8), :] for c in range(3)]
    along_z = [shift_z(center[c]) for c in range(3)]
    return center, (along_x, along_y, along_z)


def stress_rows(field, plane, tau, tau_plane, row):
    _, d = differences(field, plane, row)
    xy, xz, yz = d[0][1] + d[1][0], d[0][2] + d[2][0], d[1][2] + d[2][1]
    diagonal = d[0][0] * d[0][0] + d[1][1] * d[1][1] + d[2][2] * d[2][2]
    mixed = xy * xy + xz * xz + yz * yz
    nu = 0.05 + 0.04 * jnp.sqrt(0.5 * diagonal + 0.25 * mixed)
    half = -0.5 * nu
    rows = pl.ds(row, 8)
    for c in range(3):
        tau[c, tau_plane, rows, :] = -nu * d[c][c]
    tau[3, tau_plane, rows, :] = half * xy
    tau[4, tau_plane, rows, :] = half * xz
    tau[5, tau_plane, rows, :] = half * yz


def step_rows(field, plane, tau, tau_plane, row):
    center, d = differences(field, plane, row)
    here = pl.ds(row, 8)

    def tau_x(c):
        return tau[c, tau_plane + 1, here, :] - tau[c, tau_plane - 1, here, :]

    def tau_y(c):
        return tau[c, tau_plane, pl.ds(row + 1, 8), :] - tau[c, tau_plane, pl.ds(row - 1, 8), :]

    below = wall_stress([value[:, :128] for value in center])
    above = wall_stress([-value[:, 384:] for value in center])

    def tau_z(c):
        return shift_z(tau[c, tau_plane, here, :], below[c], above[c])

    parts = ((0, 3, 4), (3, 1, 5), (4, 5, 2))
    out = []
    for j in range(3):
        a, b, c = parts[j]
        total = tau_x(a) + tau_y(b) + tau_z(c)
        total += center[0] * d[0][j] + center[1] * d[1][j] + center[2] * d[2][j]
        new = center[j] - 0.05 * total
        out.append(new + 0.005 if j == 0 else new)
    return out


def add_columns(tile, tile_target, starts, weights, totals):
    w1, w2, w2t, w3, w3t = weights
    g1, g2, g3 = totals
    columns, targets = [], []
    for n, first in enumerate(starts):
        start = first + 127
        base_lane = pl.multiple_of(lax.shift_right_logical(start, 7) * 128, 128)
        turn = (512 - (start & 127)) & 511
        window = pltpu.roll(tile[n * 32 : n * 32 + 32, pl.ds(base_lane, 512)], turn, 1)
        columns.append(jnp.concatenate([window[:, 0:256], window[:, 1:257], window[:, 2:258]], 0))
        target = pltpu.roll(tile_target[n * 16 : n * 16 + 16, pl.ds(base_lane, 512)], turn, 1)
        targets.append(target[:, 1:257])
    half = len(starts) // 2
    cols = [jnp.concatenate(columns[:half], 1), jnp.concatenate(columns[half:], 1)]
    target = jnp.concatenate([jnp.concatenate(targets[:half], 1), jnp.concatenate(targets[half:], 1)], 0)
    h1 = jnp.concatenate([dot(w1[...], cols[0]), dot(w1[...], cols[1])], 0)
    t1 = jnp.tanh(h1)
    q1 = h1 * t1
    a1 = (h1 + q1).astype(bf16)
    s1 = (1.0 + t1) * (1.0 + (h1 - q1))
    h2 = dot(w2[...], a1)
    t2 = jnp.tanh(h2)
    q2 = h2 * t2
    a2 = (h2 + q2).astype(bf16)
    s2 = (1.0 + t2) * (1.0 + (h2 - q2))
    misfit = (dot(w3[...], a2) - target.astype(f32)).astype(bf16)
    b2 = (dot(w3t[...], misfit) * s2).astype(bf16)
    b1 = (dot(w2t[...], b2) * s1).astype(bf16)
    g3[...] += dot_cells(side_by_side(misfit), side_by_side(a2))
    both = dot_cells(b2, a1)
    g2[...] += both[0:64, 0:64] + both[64:128, 64:128]
    g1[...] += dot_cells(side_by_side(b1), jnp.concatenate(cols, 1))


def side_by_side(value):
    half = value.shape[0] // 2
    return jnp.concatenate([value[:half], value[half:]], 1)


def input_rows(field, plane):
    rows = [field[c, plane + ox - 1, 8:32, 0:512] for c in range(3) for ox in range(3)]
    return jnp.concatenate(rows, 0).astype(bf16)


def target_rows(tau, plane):
    return jnp.concatenate([tau[c, plane, 12:28, 0:512].astype(bf16) for c in range(6)], 0)


def gather(tile, at, table, rows):
    tile[at : at + table.shape[0], 128:640] = dot(table, rows).astype(bf16)


def clear_edges(*tiles):
    for tile in tiles:
        edge = jnp.zeros((tile.shape[0], 128), bf16)
        tile[:, 0:128] = edge
        tile[:, 640:768] = edge


def clear_rest(field):
    strip = jnp.zeros((8, LANES), f32)
    for c in range(3):
        for p in range(field.shape[1]):
            field[c, p, 4:12, :] = strip
            field[c, p, 28:36, :] = strip


def twice(block):
    zero = jnp.zeros_like(block)
    return jnp.concatenate([jnp.concatenate([block, zero], 1), jnp.concatenate([zero, block], 1)], 0)


def interior_kernel(
    offs, own, first, mid, last, table, packed_weights, packed_totals, field, tau, tile, tile_target,
    local_table, local_first, local_mid, local_last, sems,
):
    pairs_in = ((first, local_first), (mid, local_mid), (last, local_last), (table, local_table))
    copies = [pltpu.make_async_copy(a, b, sems.at[k]) for k, (a, b) in enumerate(pairs_in)]
    for copy in copies:
        copy.start()
    clear_edges(tile, tile_target)
    clear_rest(field)
    for c in range(3):
        for p in range(4):
            field[c, p, 12:28, 0:512] = own[c, p]
    for copy in copies:
        copy.wait()
    first, mid, last = local_first, local_mid, local_last
    pick, pick_target, order = table_parts(local_table)
    weights, totals = weight_parts(packed_weights), total_parts(packed_totals)
    w1, w2, w2t, w3, w3t = weights
    rows, cols = lax.broadcasted_iota(jnp.int32, (64, 64), 0), lax.broadcasted_iota(jnp.int32, (64, 64), 1)
    half = jnp.where(rows == cols, 0.5, 0.0).astype(bf16)
    w1[...] = (0.5 * dot(first[...], order[...])).astype(bf16)
    w2[...] = twice(0.5 * mid[...].astype(f32)).astype(bf16)
    w2t[...] = twice(dot_cells(half, mid[...])).astype(bf16)
    last_rows = jnp.concatenate([last[...].astype(f32), jnp.zeros((10, 64), f32)], 0)
    w3[...] = twice(last_rows).astype(bf16)
    w3t[...] = twice(dot_cells(half, last_rows.astype(bf16))).astype(bf16)
    packed_totals[...] = jnp.zeros_like(packed_totals)

    def step(n, _):
        x = n + 1
        for row in (12, 20):
            stress_rows(field, x, tau, n, row)
        gather(tile, 0, pick[...], input_rows(field, x))
        gather(tile_target, 0, pick_target[...], target_rows(tau, n))
        starts = [offs[x, y] for y in range(1, 15)]
        add_columns(tile.at[32:480], tile_target.at[16:240], starts, weights, totals)
        return 0

    lax.fori_loop(0, 2, step, 0)


def split_bf16(value):
    high = value.astype(bf16)
    return high, (value - high.astype(f32)).astype(bf16)


def in_order(axis, step, first, second):
    odd = lax.axis_index(axis) % 2

    @pl.when(odd == 1)
    def _():
        step(first, second)

    @pl.when(odd == 0)
    def _():
        step(second, first)


def pack_x_kernel(own, first, second):
    def pack(down, up):
        for c in range(3):
            for x in range(4):
                high, rest = split_bf16(own[c, x])
                up[c, x] = high
                down[c, x + 1] = high
                if x == 3:
                    up[c, 4] = rest
                if x == 0:
                    down[c, 0] = rest

    in_order("px", pack, first, second)


def pack_y_kernel(own, x_first, x_second, first, second):
    def pack(x_low, x_high, left, right):
        for c in range(3):
            for out, start, near in ((right, 12, 15), (left, 0, 0)):
                rests = []
                for p in range(12):
                    if p < 4:
                        high = x_low[c, p].astype(f32)
                    elif p < 8:
                        high, rest = split_bf16(own[c, p - 4])
                        high, rest = high.astype(f32), rest.astype(f32)
                    else:
                        high = x_high[c, p - 7].astype(f32)
                    if p == 3:
                        rest = x_low[c, 4].astype(f32)
                    if p == 8:
                        rest = x_high[c, 0].astype(f32)
                    out[c, p] = high[start : start + 4, :].astype(bf16)
                    if 3 <= p <= 8:
                        rests.append(rest[near : near + 1, :])
                rests = jnp.concatenate(rests + [jnp.zeros((2, 512), f32)], 0)
                out[c, 12] = rests[0:4].astype(bf16)
                out[c, 13] = rests[4:8].astype(bf16)

    def with_x(x_low, x_high):
        in_order("py", lambda left, right: pack(x_low, x_high, left, right), first, second)

    in_order("px", with_x, x_first, x_second)


def x_plane(x_low, own, x_high, c, p):
    if p < 4:
        plane = x_low[c, p].astype(f32)
        return plane + x_low[c, 4].astype(f32) if p == 3 else plane
    if p < 8:
        return own[c, p - 4]
    plane = x_high[c, p - 7].astype(f32)
    return plane + x_high[c, 0].astype(f32) if p == 8 else plane


def side_kernel(
    offs, own, x_first, x_second, packed_weights, before, table, packed_totals, field, tau, tile, tile_target,
    local_table, sems,
):
    copy = pltpu.make_async_copy(table, local_table, sems.at[0])
    copy.start()
    pick, pick_target, _ = table_parts(local_table)
    weights, totals = weight_parts(packed_weights), total_parts(packed_totals)
    packed_totals[...] = before[...]
    clear_edges(tile, tile_target)
    clear_rest(field)

    def place(x_low, x_high):
        for c in range(3):
            for p in range(6):
                field[c, p, 12:28, 0:512] = x_plane(x_low, own, x_high, c, p + 3)

    in_order("px", place, x_first, x_second)
    copy.wait()

    def step(n, _):
        x = 3 * n
        for row in (12, 20):
            stress_rows(field, x + 1, tau, 0, row)
        gather(tile, 0, pick[...], input_rows(field, x + 1))
        gather(tile_target, 0, pick_target[...], target_rows(tau, 0))
        starts = [offs[x, y] for y in range(1, 15)]
        add_columns(tile.at[32:480], tile_target.at[16:240], starts, weights, totals)
        return 0

    lax.fori_loop(0, 2, step, 0)


def middle_kernel(
    offs, own, x_first, x_second, y_first, y_second,
    packed_weights, before, table, middle, packed, field, tau, tile, tile_target,
    local_table, sems, packed_totals,
):
    copy = pltpu.make_async_copy(table, local_table, sems.at[0])
    copy.start()
    pick, pick_target, order = table_parts(local_table)
    weights, totals = weight_parts(packed_weights), total_parts(packed_totals)
    packed_totals[...] = before[...]
    edges, edges_target = edge_parts(local_table)
    g1, g2, g3 = totals
    clear_edges(tile, tile_target)
    clear_rest(field)
    line = jnp.zeros((1, LANES), f32)
    for c in range(6):
        for p in range(10):
            tau[c, p, 7:8, :] = line
            tau[c, p, 32:33, :] = line
    def place_x(x_low, x_high):
        for c in range(3):
            for p in range(12):
                field[c, p, 12:28, 0:512] = x_plane(x_low, own, x_high, c, p)

    def place_y(y_low, y_high):
        for c in range(3):
            for p in range(12):
                low, high = y_low[c, p].astype(f32), y_high[c, p].astype(f32)
                field[c, p, 8:12, 0:512] = low
                field[c, p, 28:32, 0:512] = high
                if 3 <= p <= 8:
                    k, r = 12 + (p - 3) // 4, (p - 3) % 4
                    field[c, p, 11:12, 0:512] = low[3:4] + y_low[c, k].astype(f32)[r : r + 1]
                    field[c, p, 28:29, 0:512] = high[0:1] + y_high[c, k].astype(f32)[r : r + 1]

    in_order("px", place_x, x_first, x_second)
    in_order("py", place_y, y_first, y_second)

    def stress_zero(p, _):
        for row in (8, 16, 24):
            stress_rows(field, p + 1, tau, p, row)
        return 0

    lax.fori_loop(0, 10, stress_zero, 0, unroll=5)

    def advance_middle(p, _):
        for row in (8, 16, 24):
            new = step_rows(field, p + 2, tau, p + 1, row)
            for c in range(3):
                middle[c, p, pl.ds(row, 8), :] = new[c]
        return 0

    lax.fori_loop(0, 8, advance_middle, 0, unroll=4)
    copy.wait()

    def step(x, _):
        gather(tile, 512, edges[...], input_rows(field, x + 4))
        gather(tile_target, 256, edges_target[...], target_rows(tau, x + 3))
        for row in (12, 20):
            stress_rows(middle, x + 2, tau, 0, row)
        gather(tile, 0, pick[...], input_rows(middle, x + 2))
        gather(tile_target, 0, pick_target[...], target_rows(tau, 0))
        starts = [offs[x, y] for y in range(16)] + [offs[x, 0], offs[x, 15]]
        add_columns(tile, tile_target, starts, weights, totals)
        return 0

    lax.fori_loop(0, 4, step, 0)
    scale = 0.5**22
    ordered = lax.dot_general(
        g1[...], order[...].astype(f32), NT, preferred_element_type=f32, precision=lax.Precision.HIGHEST
    )
    mids = g2[...]
    packed[0:64, :] = scale * jnp.concatenate([ordered, jnp.zeros((64, 15), f32), mids[:, 0:32]], 1)
    packed[64:80, :] = scale * jnp.concatenate([mids[16 * k : 16 * k + 16, 32:64] for k in range(4)], 1)
    packed[80:88, :] = scale * jnp.concatenate([g3[...][0:8], jnp.zeros((8, 64), f32)], 1)


def final_kernel(middle, final, tau):
    def stress_one(p, _):
        for row in (8, 16, 24):
            stress_rows(middle, p + 1, tau, p, row)
        return 0

    lax.fori_loop(0, 6, stress_one, 0, unroll=3)

    def advance_final(p, _):
        for row in (12, 20):
            new = step_rows(middle, p + 2, tau, p + 1, row)
            for c in range(3):
                final[c, p, row - 12 : row - 4, :] = new[c]
        return 0

    lax.fori_loop(0, 4, advance_final, 0, unroll=2)


def last_sum_kernel(a, b, c, d, first, mid, last):
    total = (a[...] + b[...]) + (c[...] + d[...])
    first[...] = total[0:64, 0:81]
    rest = jnp.concatenate([total[64:80, 32 * k : 32 * k + 32] for k in range(4)], 0)
    mid[...] = jnp.concatenate([total[0:64, 96:128], rest], 1)
    last[...] = total[80:86, 0:64]


def shaped(*dims, kind=f32):
    return jax.ShapeDtypeStruct(dims, kind)


WEIGHTS, TOTALS = shaped(480, 128, kind=bf16), shaped(144, 128)


def call(kernel, args, out_shape, scratch, smem=0, us=1, mib=16, hbm=0):
    vmem = pl.BlockSpec(memory_space=pltpu.VMEM)
    scalar = pl.BlockSpec(memory_space=pltpu.SMEM)
    far = pl.BlockSpec(memory_space=pltpu.HBM)
    return pl.pallas_call(
        kernel,
        in_specs=[scalar] * smem + [vmem] * (len(args) - smem - hbm) + [far] * hbm,
        out_specs=[vmem] * len(out_shape),
        out_shape=out_shape,
        scratch_shapes=scratch,
        compiler_params=pltpu.CompilerParams(vmem_limit_bytes=mib * 2**20),
        cost_estimate=pl.CostEstimate(flops=int(us * 1.15e9), bytes_accessed=int(us * 3.69e6), transcendentals=0),
    )(*args)


def columns_scratch(planes, stress_planes, columns):
    return [
        pltpu.VMEM((3, planes, ROWS, LANES), f32),
        pltpu.VMEM((6, stress_planes, ROWS, LANES), f32),
        pltpu.VMEM((32 * columns, 768), bf16),
        pltpu.VMEM((16 * columns, 768), bf16),
        pltpu.VMEM((960, 216), bf16),
    ]


def pairs(move):
    return [(i * 16 + j, (move(i, j)[0] % 8) * 16 + move(i, j)[1] % 16) for i in range(8) for j in range(16)]


EXCHANGES = (lambda k: k ^ 1, lambda k: k ^ 3, lambda k: k ^ 2)


def along_y(turn):
    return lambda i, j: (i & 4 | turn(i & 3), j)


def along_x(turn):
    return lambda i, j: (i, j & 9 | turn(j >> 1 & 3) << 1)


def along_z(turn):
    def move(i, j):
        z = turn((j >> 3) * 2 + (i >> 2))
        return ((z & 1) * 4 + (i & 3), (z >> 1) * 8 + (j & 7))

    return move


def send(value, move):
    return lax.ppermute(value, AXES, pairs(move))


def body(velocity, first_weight, mid_weight, last_weight, offsets):
    table = jnp.asarray(selections(), bf16)
    near_x, far_x = lambda i, j: (i ^ 1, j), lambda i, j: (i + 2 * (i % 2) - 1, j)
    near_y, far_y = lambda i, j: (i, j ^ 1), lambda i, j: (i, j + 2 * (j % 2) - 1)
    to_near, to_far = call(pack_x_kernel, (velocity,), [shaped(3, 5, 16, 512, kind=bf16)] * 2, [])
    x_first, x_second = send(to_near, near_x), send(to_far, far_x)
    weights, totals = call(
        interior_kernel,
        (offsets, velocity, first_weight, mid_weight, last_weight, table),
        [WEIGHTS, TOTALS], columns_scratch(4, 2, 16)
        + [pltpu.VMEM(n, bf16) for n in ((64, 81), (64, 64), (6, 64))] + [pltpu.SemaphoreType.DMA((4,))],
        1, 6, 16, 4,
    )
    x_first, x_second, totals = lax.optimization_barrier((x_first, x_second, totals))
    to_near, to_far = call(
        pack_y_kernel, (velocity, x_first, x_second), [shaped(3, 14, 4, 512, kind=bf16)] * 2, []
    )
    y_first, y_second = send(to_near, near_y), send(to_far, far_y)
    (totals,) = call(
        side_kernel,
        (offsets, velocity, x_first, x_second, weights, totals, table),
        [TOTALS], columns_scratch(6, 1, 16) + [pltpu.SemaphoreType.DMA((1,))], 1, 6, 16, 1,
    )
    middle, packed = call(
        middle_kernel,
        (offsets, velocity, x_first, x_second, y_first, y_second, weights, totals, table),
        [shaped(3, 8, ROWS, LANES), shaped(88, 128)],
        columns_scratch(12, 10, 18) + [pltpu.SemaphoreType.DMA((1,)), pltpu.VMEM(TOTALS.shape, f32)], 1, 16, 32, 1,
    )
    (final,) = call(final_kernel, (middle,), [shaped(3, 4, 16, 512)], [pltpu.VMEM((6, 6, ROWS, LANES), f32)], 0, 3)

    packed = packed + send(packed, near_y)
    for along in (along_y, along_x):
        a, b, c = (send(packed, along(turn)) for turn in EXCHANGES)
        packed = (packed + a) + (b + c)
    a, b, c = (send(packed, along_z(turn)) for turn in EXCHANGES)
    grads = call(last_sum_kernel, (packed, a, b, c), [shaped(64, 81), shaped(64, 64), shaped(6, 64)], [])
    return final, *grads


def solution(mesh):
    in_specs = (P(None, "px", "py", None), P(), P(), P(), P("px", "py"))
    out_specs = (P(None, "px", "py", None), P(), P(), P())
    return jax.shard_map(body, mesh=mesh, in_specs=in_specs, out_specs=out_specs, check_vma=False)
```

```python
import jax
import jax.numpy as jnp
import numpy as np
from jax import lax
from jax.experimental import pallas as pl
from jax.experimental.pallas import tpu as pltpu
from jax.sharding import PartitionSpec as P

f32, bf16 = jnp.float32, jnp.bfloat16
AXES = ("px", "py")
LANES = 512
ROWS = 40
NT = (((1,), (1,)), ((), ()))


def selections():
    table = np.zeros((960, 216), np.float32)
    for y in range(16):
        for c in range(3):
            for ox in range(3):
                for oy in range(3):
                    table[y * 32 + c * 9 + ox * 3 + oy, (c * 3 + ox) * 24 + y + oy + 3] = 1
        for c in range(6):
            table[512 + y * 16 + c, c * 16 + y] = 1
    for oz in range(3):
        for c in range(3):
            for o in range(9):
                table[768 + c * 27 + o * 3 + oz, oz * 32 + c * 9 + o] = 1
    table[864:928] = table[np.r_[0:32, 480:512]]
    table[928:960] = table[np.r_[512:528, 752:768]]
    return table


class Part:
    def __init__(self, ref, first, last, lanes):
        self.ref, self.first, self.last, self.lanes = ref, first, last, lanes

    def __getitem__(self, _):
        return self.ref[self.first : self.last, 0 : self.lanes]

    def __setitem__(self, _, value):
        self.ref[self.first : self.last, 0 : self.lanes] = value


def table_parts(table):
    return Part(table, 0, 512, 216), Part(table, 512, 768, 96), Part(table, 768, 849, 96)


def edge_parts(table):
    return Part(table, 864, 928, 216), Part(table, 928, 960, 96)


def weight_parts(packed):
    return (Part(packed, 0, 64, 96), Part(packed, 64, 192, 128), Part(packed, 192, 320, 128),
            Part(packed, 320, 352, 128), Part(packed, 352, 480, 32))


def total_parts(packed):
    return Part(packed, 0, 64, 96), Part(packed, 64, 128, 64), Part(packed, 128, 144, 64)


def dot(a, b):
    return jnp.dot(a, b, preferred_element_type=f32)


def dot_cells(a, b):
    return lax.dot_general(a, b, NT, preferred_element_type=f32)


def shift_z(value, below=0.0, above=0.0):
    up, down = pltpu.roll(value, LANES - 1, 1), pltpu.roll(value, 1, 1)
    lane = lax.broadcasted_iota(jnp.int32, (8, 128), 1)
    first = up[:, :128] - jnp.where(lane == 0, below, down[:, :128])
    last = jnp.where(lane == 127, above, up[:, 384:]) - down[:, 384:]
    return jnp.concatenate([first, up[:, 128:384] - down[:, 128:384], last], 1)


def wall_stress(velocity):
    x, y, z = velocity
    nu = 0.05 + 0.04 * jnp.sqrt(0.5 * z * z + 0.25 * (x * x + y * y))
    return {4: -0.5 * nu * x, 5: -0.5 * nu * y, 2: -nu * z}


def differences(field, plane, row):
    here = pl.ds(row, 8)
    center = [field[c, plane, here, :] for c in range(3)]
    along_x = [field[c, plane + 1, here, :] - field[c, plane - 1, here, :] for c in range(3)]
    along_y = [field[c, plane, pl.ds(row + 1, 8), :] - field[c, plane, pl.ds(row - 1, 8), :] for c in range(3)]
    along_z = [shift_z(center[c]) for c in range(3)]
    return center, (along_x, along_y, along_z)


def stress_rows(field, plane, tau, tau_plane, row):
    _, d = differences(field, plane, row)
    xy, xz, yz = d[0][1] + d[1][0], d[0][2] + d[2][0], d[1][2] + d[2][1]
    diagonal = d[0][0] * d[0][0] + d[1][1] * d[1][1] + d[2][2] * d[2][2]
    mixed = xy * xy + xz * xz + yz * yz
    nu = 0.05 + 0.04 * jnp.sqrt(0.5 * diagonal + 0.25 * mixed)
    half = -0.5 * nu
    rows = pl.ds(row, 8)
    for c in range(3):
        tau[c, tau_plane, rows, :] = -nu * d[c][c]
    tau[3, tau_plane, rows, :] = half * xy
    tau[4, tau_plane, rows, :] = half * xz
    tau[5, tau_plane, rows, :] = half * yz


def step_rows(field, plane, tau, tau_plane, row):
    center, d = differences(field, plane, row)
    here = pl.ds(row, 8)

    def tau_x(c):
        return tau[c, tau_plane + 1, here, :] - tau[c, tau_plane - 1, here, :]

    def tau_y(c):
        return tau[c, tau_plane, pl.ds(row + 1, 8), :] - tau[c, tau_plane, pl.ds(row - 1, 8), :]

    below = wall_stress([value[:, :128] for value in center])
    above = wall_stress([-value[:, 384:] for value in center])

    def tau_z(c):
        return shift_z(tau[c, tau_plane, here, :], below[c], above[c])

    parts = ((0, 3, 4), (3, 1, 5), (4, 5, 2))
    out = []
    for j in range(3):
        a, b, c = parts[j]
        total = tau_x(a) + tau_y(b) + tau_z(c)
        total += center[0] * d[0][j] + center[1] * d[1][j] + center[2] * d[2][j]
        new = center[j] - 0.05 * total
        out.append(new + 0.005 if j == 0 else new)
    return out


def add_columns(tile, tile_target, starts, weights, totals):
    w1, w2, w2t, w3, w3t = weights
    g1, g2, g3 = totals
    columns, targets = [], []
    for n, first in enumerate(starts):
        start = first + 127
        base_lane = pl.multiple_of(lax.shift_right_logical(start, 7) * 128, 128)
        turn = (512 - (start & 127)) & 511
        window = pltpu.roll(tile[n * 32 : n * 32 + 32, pl.ds(base_lane, 512)], turn, 1)
        columns.append(jnp.concatenate([window[:, 0:256], window[:, 1:257], window[:, 2:258]], 0))
        target = pltpu.roll(tile_target[n * 16 : n * 16 + 16, pl.ds(base_lane, 512)], (turn - 1) & 511, 1)
        targets.append(target[:, 0:256])
    half = len(starts) // 2
    cols = [jnp.concatenate(columns[:half], 1), jnp.concatenate(columns[half:], 1)]
    target = jnp.concatenate([jnp.concatenate(targets[:half], 1), jnp.concatenate(targets[half:], 1)], 0)
    h1 = jnp.concatenate([dot(w1[...], cols[0]), dot(w1[...], cols[1])], 0)
    t1 = jnp.tanh(h1)
    q1 = h1 * t1
    a1 = (h1 + q1).astype(bf16)
    s1 = (1.0 + t1) * (1.0 + (h1 - q1))
    h2 = dot(w2[...], a1)
    t2 = jnp.tanh(h2)
    q2 = h2 * t2
    a2 = (h2 + q2).astype(bf16)
    s2 = (1.0 + t2) * (1.0 + (h2 - q2))
    misfit = (dot(w3[...], a2) - target.astype(f32)).astype(bf16)
    b2 = (dot(w3t[...], misfit) * s2).astype(bf16)
    b1 = (dot(w2t[...], b2) * s1).astype(bf16)
    g3[...] += dot_cells(side_by_side(misfit), side_by_side(a2))
    both = dot_cells(b2, a1)
    g2[...] += both[0:64, 0:64] + both[64:128, 64:128]
    g1[...] += dot_cells(side_by_side(b1), jnp.concatenate(cols, 1))


def side_by_side(value):
    half = value.shape[0] // 2
    return jnp.concatenate([value[:half], value[half:]], 1)


def input_rows(field, plane):
    rows = [field[c, plane + ox - 1, 8:32, 0:512] for c in range(3) for ox in range(3)]
    return jnp.concatenate(rows, 0).astype(bf16)


def target_rows(tau, plane):
    return jnp.concatenate([tau[c, plane, 12:28, 0:512].astype(bf16) for c in range(6)], 0)


def gather(tile, at, table, rows):
    tile[at : at + table.shape[0], 128:640] = dot(table, rows).astype(bf16)


def clear_edges(*tiles):
    for tile in tiles:
        edge = jnp.zeros((tile.shape[0], 128), bf16)
        tile[:, 0:128] = edge
        tile[:, 640:768] = edge


def clear_rest(field):
    strip = jnp.zeros((8, LANES), f32)
    for c in range(3):
        for p in range(field.shape[1]):
            field[c, p, 4:12, :] = strip
            field[c, p, 28:36, :] = strip


def twice(block):
    zero = jnp.zeros_like(block)
    return jnp.concatenate([jnp.concatenate([block, zero], 1), jnp.concatenate([zero, block], 1)], 0)


def interior_kernel(
    offs, own, first, mid, last, table, packed_weights, packed_totals, field, tau, tile, tile_target,
    local_table, local_first, local_mid, local_last, sems,
):
    pairs_in = ((first, local_first), (mid, local_mid), (last, local_last), (table, local_table))
    copies = [pltpu.make_async_copy(a, b, sems.at[k]) for k, (a, b) in enumerate(pairs_in)]
    for copy in copies:
        copy.start()
    clear_edges(tile, tile_target)
    clear_rest(field)
    for c in range(3):
        for p in range(4):
            field[c, p, 12:28, 0:512] = own[c, p]
    for copy in copies:
        copy.wait()
    first, mid, last = local_first, local_mid, local_last
    pick, pick_target, order = table_parts(local_table)
    weights, totals = weight_parts(packed_weights), total_parts(packed_totals)
    w1, w2, w2t, w3, w3t = weights
    rows, cols = lax.broadcasted_iota(jnp.int32, (64, 64), 0), lax.broadcasted_iota(jnp.int32, (64, 64), 1)
    half = jnp.where(rows == cols, 0.5, 0.0).astype(bf16)
    w1[...] = (0.5 * dot(first[...], order[...])).astype(bf16)
    w2[...] = twice(0.5 * mid[...].astype(f32)).astype(bf16)
    w2t[...] = twice(dot_cells(half, mid[...])).astype(bf16)
    last_rows = jnp.concatenate([last[...].astype(f32), jnp.zeros((10, 64), f32)], 0)
    w3[...] = twice(last_rows).astype(bf16)
    w3t[...] = twice(dot_cells(half, last_rows.astype(bf16))).astype(bf16)
    packed_totals[...] = jnp.zeros_like(packed_totals)

    starts = []
    for n in range(2):
        x = n + 1
        for row in (12, 20):
            stress_rows(field, x, tau, n, row)
        gather(tile, 448 * n, pick.ref[32:480, :], input_rows(field, x))
        gather(tile_target, 224 * n, pick_target.ref[528:752, 0:96], target_rows(tau, n))
        starts += [offs[x, y] for y in range(1, 15)]
    add_columns(tile, tile_target, starts, weights, totals)


def split_bf16(value):
    high = value.astype(bf16)
    return high, (value - high.astype(f32)).astype(bf16)


def in_order(axis, step, first, second):
    odd = lax.axis_index(axis) % 2

    @pl.when(odd == 0)
    def _():
        step(first, second)

    @pl.when(odd == 1)
    def _():
        step(second, first)


def pack_x_kernel(own, first, second):
    def pack(down, up):
        for c in range(3):
            for x in range(4):
                high, rest = split_bf16(own[c, x])
                up[c, x] = high
                down[c, x + 1] = high
                if x == 3:
                    up[c, 4] = rest
                if x == 0:
                    down[c, 0] = rest

    in_order("px", pack, first, second)


def pack_y_kernel(own, x_first, x_second, first, second):
    def pack(x_low, x_high, left, right):
        for c in range(3):
            for out, at_top in ((right, True), (left, False)):

                def rows(p, count):
                    plane = x_low[c, p] if p < 4 else own[c, p - 4] if p < 8 else x_high[c, p - 7]
                    return plane.astype(f32)[16 - count :] if at_top else plane.astype(f32)[:count]

                def rest(p):
                    if p == 3 or p == 8:
                        plane = (x_low[c, 4] if p == 3 else x_high[c, 0]).astype(f32)
                    else:
                        plane = split_bf16(own[c, p - 4])[1].astype(f32)
                    return plane[15:] if at_top else plane[:1]

                blocks = [[rows(p, 4)] for p in range(4, 8)]
                blocks += [[rows(3, 3), rows(1, 1)], [rows(8, 3), rows(10, 1)], [rows(2, 2), rows(9, 2)]]
                blocks += [[rest(p) for p in range(3, 7)], [rest(7), rest(8), jnp.zeros((2, 512), f32)]]
                for k, block in enumerate(blocks):
                    out[c, k] = jnp.concatenate(block, 0).astype(bf16)

    def with_x(x_low, x_high):
        in_order("py", lambda left, right: pack(x_low, x_high, left, right), first, second)

    in_order("px", with_x, x_first, x_second)


def x_plane(x_low, own, x_high, c, p):
    if p < 4:
        plane = x_low[c, p].astype(f32)
        return plane + x_low[c, 4].astype(f32) if p == 3 else plane
    if p < 8:
        return own[c, p - 4]
    plane = x_high[c, p - 7].astype(f32)
    return plane + x_high[c, 0].astype(f32) if p == 8 else plane


def side_kernel(
    offs, own, x_first, x_second, packed_weights, before, table, packed_totals, field, tau, tile, tile_target,
    local_table, sems,
):
    copy = pltpu.make_async_copy(table, local_table, sems.at[0])
    copy.start()
    pick, pick_target, _ = table_parts(local_table)
    weights, totals = weight_parts(packed_weights), total_parts(packed_totals)
    packed_totals[...] = before[...]
    clear_edges(tile, tile_target)
    clear_rest(field)

    def place(x_low, x_high):
        for c in range(3):
            for p in range(6):
                field[c, p, 12:28, 0:512] = x_plane(x_low, own, x_high, c, p + 3)

    in_order("px", place, x_first, x_second)
    copy.wait()

    starts = []
    for n in range(2):
        x = 3 * n
        for row in (12, 20):
            stress_rows(field, x + 1, tau, n, row)
        gather(tile, 448 * n, pick.ref[32:480, :], input_rows(field, x + 1))
        gather(tile_target, 224 * n, pick_target.ref[528:752, 0:96], target_rows(tau, n))
        starts += [offs[x, y] for y in range(1, 15)]
    add_columns(tile, tile_target, starts, weights, totals)


def middle_kernel(
    offs, own, x_first, x_second, y_first, y_second,
    packed_weights, before, table, middle, packed, field, tau, tile, tile_target,
    local_table, sems, packed_totals,
):
    copy = pltpu.make_async_copy(table, local_table, sems.at[0])
    copy.start()
    pick, pick_target, order = table_parts(local_table)
    weights, totals = weight_parts(packed_weights), total_parts(packed_totals)
    packed_totals[...] = before[...]
    edges, edges_target = edge_parts(local_table)
    g1, g2, g3 = totals
    clear_edges(tile, tile_target)
    clear_rest(field)
    line = jnp.zeros((1, LANES), f32)
    for c in range(6):
        for p in range(10):
            tau[c, p, 7:8, :] = line
            tau[c, p, 32:33, :] = line
    def place_x(x_low, x_high):
        for c in range(3):
            for p in range(12):
                field[c, p, 12:28, 0:512] = x_plane(x_low, own, x_high, c, p)

    def place_y(y_low, y_high):
        parts = [(p, 4, p - 4, 0) for p in range(4, 8)]
        parts += [(3, 3, 4, 0), (1, 1, 4, 3), (8, 3, 5, 0), (10, 1, 5, 3), (2, 2, 6, 0), (9, 2, 6, 2)]
        for c in range(3):
            for p, count, k, at in parts:
                low = y_low[c, k].astype(f32)[at : at + count]
                high = y_high[c, k].astype(f32)[at : at + count]
                field[c, p, 12 - count : 12, 0:512] = low
                field[c, p, 28 : 28 + count, 0:512] = high
                if 3 <= p <= 8:
                    k, at = 7 + (p - 3) // 4, (p - 3) % 4
                    field[c, p, 11:12, 0:512] = low[count - 1 :] + y_low[c, k].astype(f32)[at : at + 1]
                    field[c, p, 28:29, 0:512] = high[:1] + y_high[c, k].astype(f32)[at : at + 1]

    in_order("px", place_x, x_first, x_second)
    in_order("py", place_y, y_first, y_second)

    def stress_zero(p, _):
        for row in (8, 16, 24):
            stress_rows(field, p + 1, tau, p, row)
        return 0

    lax.fori_loop(0, 10, stress_zero, 0, unroll=5)

    def advance_middle(p, _):
        for row in (8, 16, 24):
            new = step_rows(field, p + 2, tau, p + 1, row)
            for c in range(3):
                middle[c, p, pl.ds(row, 8), :] = new[c]
        return 0

    lax.fori_loop(0, 8, advance_middle, 0, unroll=4)
    copy.wait()

    def step(x, _):
        gather(tile, 512, edges[...], input_rows(field, x + 4))
        gather(tile_target, 256, edges_target[...], target_rows(tau, x + 3))
        for row in (12, 20):
            stress_rows(middle, x + 2, tau, 0, row)
        gather(tile, 0, pick[...], input_rows(middle, x + 2))
        gather(tile_target, 0, pick_target[...], target_rows(tau, 0))
        starts = [offs[x, y] for y in range(16)] + [offs[x, 0], offs[x, 15]]
        add_columns(tile, tile_target, starts, weights, totals)
        return 0

    lax.fori_loop(0, 4, step, 0)
    scale = 0.5**22
    ordered = lax.dot_general(
        g1[...], order[...].astype(f32), NT, preferred_element_type=f32, precision=lax.Precision.HIGHEST
    )
    mids = g2[...]
    packed[0:64, :] = scale * jnp.concatenate([ordered, jnp.zeros((64, 15), f32), mids[:, 0:32]], 1)
    packed[64:80, :] = scale * jnp.concatenate([mids[16 * k : 16 * k + 16, 32:64] for k in range(4)], 1)
    packed[80:88, :] = scale * jnp.concatenate([g3[...][0:8], jnp.zeros((8, 64), f32)], 1)


def final_kernel(middle, final, tau):
    def stress_one(p, _):
        for row in (8, 16, 24):
            stress_rows(middle, p + 1, tau, p, row)
        return 0

    lax.fori_loop(0, 6, stress_one, 0, unroll=3)

    def advance_final(p, _):
        for row in (12, 20):
            new = step_rows(middle, p + 2, tau, p + 1, row)
            for c in range(3):
                final[c, p, row - 12 : row - 4, :] = new[c]
        return 0

    lax.fori_loop(0, 4, advance_final, 0, unroll=2)


def last_sum_kernel(a, b, c, d, first, mid, last):
    total = (a[...] + b[...]) + (c[...] + d[...])
    first[...] = total[0:64, 0:81]
    rest = jnp.concatenate([total[64:80, 32 * k : 32 * k + 32] for k in range(4)], 0)
    mid[...] = jnp.concatenate([total[0:64, 96:128], rest], 1)
    last[...] = total[80:86, 0:64]


def shaped(*dims, kind=f32):
    return jax.ShapeDtypeStruct(dims, kind)


WEIGHTS, TOTALS = shaped(480, 128, kind=bf16), shaped(144, 128)


def call(kernel, args, out_shape, scratch, smem=0, us=1, mib=16, hbm=0):
    vmem = pl.BlockSpec(memory_space=pltpu.VMEM)
    scalar = pl.BlockSpec(memory_space=pltpu.SMEM)
    far = pl.BlockSpec(memory_space=pltpu.HBM)
    return pl.pallas_call(
        kernel,
        in_specs=[scalar] * smem + [vmem] * (len(args) - smem - hbm) + [far] * hbm,
        out_specs=[vmem] * len(out_shape),
        out_shape=out_shape,
        scratch_shapes=scratch,
        compiler_params=pltpu.CompilerParams(vmem_limit_bytes=mib * 2**20),
        cost_estimate=pl.CostEstimate(flops=int(us * 1.15e9), bytes_accessed=int(us * 3.69e6), transcendentals=0),
    )(*args)


def columns_scratch(planes, stress_planes, columns):
    return [
        pltpu.VMEM((3, planes, ROWS, LANES), f32),
        pltpu.VMEM((6, stress_planes, ROWS, LANES), f32),
        pltpu.VMEM((32 * columns, 768), bf16),
        pltpu.VMEM((16 * columns, 768), bf16),
        pltpu.VMEM((960, 216), bf16),
    ]


def pairs(move):
    return [(i * 16 + j, (move(i, j)[0] % 8) * 16 + move(i, j)[1] % 16) for i in range(8) for j in range(16)]


EXCHANGES = (lambda k: k ^ 1, lambda k: k ^ 3, lambda k: k ^ 2)


def along_y(turn):
    return lambda i, j: (i & 4 | turn(i & 3), j)


def along_x(turn):
    return lambda i, j: (i, j & 9 | turn(j >> 1 & 3) << 1)


def along_z(turn):
    def move(i, j):
        z = turn((j >> 3) * 2 + (i >> 2))
        return ((z & 1) * 4 + (i & 3), (z >> 1) * 8 + (j & 7))

    return move


def send(value, move):
    return lax.ppermute(value, AXES, pairs(move))


def body(velocity, first_weight, mid_weight, last_weight, offsets):
    table = jnp.asarray(selections(), bf16)
    near_x, far_x = lambda i, j: (i ^ 1, j), lambda i, j: (i + 2 * (i % 2) - 1, j)
    near_y, far_y = lambda i, j: (i, j ^ 1), lambda i, j: (i, j + 2 * (j % 2) - 1)
    to_far, to_near = call(pack_x_kernel, (velocity,), [shaped(3, 5, 16, 512, kind=bf16)] * 2, [])
    x_first, x_second = send(to_far, far_x), send(to_near, near_x)
    weights, totals = call(
        interior_kernel,
        (offsets, velocity, first_weight, mid_weight, last_weight, table),
        [WEIGHTS, TOTALS], columns_scratch(4, 2, 28)
        + [pltpu.VMEM(n, bf16) for n in ((64, 81), (64, 64), (6, 64))] + [pltpu.SemaphoreType.DMA((4,))],
        1, 6, 28, 4,
    )
    x_first, x_second, totals = lax.optimization_barrier((x_first, x_second, totals))
    to_far, to_near = call(
        pack_y_kernel, (velocity, x_first, x_second), [shaped(3, 9, 4, 512, kind=bf16)] * 2, []
    )
    y_first, y_second = send(to_far, far_y), send(to_near, near_y)
    (totals,) = call(
        side_kernel,
        (offsets, velocity, x_first, x_second, weights, totals, table),
        [TOTALS], columns_scratch(6, 2, 28) + [pltpu.SemaphoreType.DMA((1,))], 1, 6, 28, 1,
    )
    middle, packed = call(
        middle_kernel,
        (offsets, velocity, x_first, x_second, y_first, y_second, weights, totals, table),
        [shaped(3, 8, ROWS, LANES), shaped(88, 128)],
        columns_scratch(12, 10, 18) + [pltpu.SemaphoreType.DMA((1,)), pltpu.VMEM(TOTALS.shape, f32)], 1, 16, 32, 1,
    )
    (final,) = call(final_kernel, (middle,), [shaped(3, 4, 16, 512)], [pltpu.VMEM((6, 6, ROWS, LANES), f32)], 0, 3)

    packed = packed + send(packed, near_y)
    for along in (along_y, along_x):
        a, b, c = (send(packed, along(turn)) for turn in EXCHANGES)
        packed = (packed + a) + (b + c)
    a, b, c = (send(packed, along_z(turn)) for turn in EXCHANGES)
    grads = call(last_sum_kernel, (packed, a, b, c), [shaped(64, 81), shaped(64, 64), shaped(6, 64)], [])
    return final, *grads


def solution(mesh):
    in_specs = (P(None, "px", "py", None), P(), P(), P(), P("px", "py"))
    out_specs = (P(None, "px", "py", None), P(), P(), P())
    return jax.shard_map(body, mesh=mesh, in_specs=in_specs, out_specs=out_specs, check_vma=False)
```

```python
import jax
import jax.numpy as jnp
import numpy as np
from jax import lax
from jax.experimental import pallas as pl
from jax.experimental.pallas import tpu as pltpu
from jax.sharding import PartitionSpec as P

f32, bf16 = jnp.float32, jnp.bfloat16
AXES = ("px", "py")
LANES = 512
ROWS = 40
NT = (((1,), (1,)), ((), ()))


def selections():
    table = np.zeros((960, 216), np.float32)
    for y in range(16):
        for c in range(3):
            for ox in range(3):
                for oy in range(3):
                    table[y * 32 + c * 9 + ox * 3 + oy, (c * 3 + ox) * 24 + y + oy + 3] = 1
        for c in range(6):
            table[512 + y * 16 + c, c * 16 + y] = 1
    for oz in range(3):
        for c in range(3):
            for o in range(9):
                table[768 + c * 27 + o * 3 + oz, oz * 32 + c * 9 + o] = 1
    table[864:928] = table[np.r_[0:32, 480:512]]
    table[928:960] = table[np.r_[512:528, 752:768]]
    return table


class Part:
    def __init__(self, ref, first, last, lanes):
        self.ref, self.first, self.last, self.lanes = ref, first, last, lanes

    def __getitem__(self, _):
        return self.ref[self.first : self.last, 0 : self.lanes]

    def __setitem__(self, _, value):
        self.ref[self.first : self.last, 0 : self.lanes] = value


def table_parts(table):
    return Part(table, 0, 512, 216), Part(table, 512, 768, 96), Part(table, 768, 849, 96)


def edge_parts(table):
    return Part(table, 864, 928, 216), Part(table, 928, 960, 96)


def weight_parts(packed):
    return (Part(packed, 0, 64, 96), Part(packed, 64, 192, 128), Part(packed, 192, 320, 128),
            Part(packed, 320, 352, 128), Part(packed, 352, 480, 32))


def total_parts(packed):
    return Part(packed, 0, 64, 96), Part(packed, 64, 128, 64), Part(packed, 128, 144, 64)


def dot(a, b):
    return jnp.dot(a, b, preferred_element_type=f32)


def dot_cells(a, b):
    return lax.dot_general(a, b, NT, preferred_element_type=f32)


def shift_z(value, below=0.0, above=0.0):
    up, down = pltpu.roll(value, LANES - 1, 1), pltpu.roll(value, 1, 1)
    lane = lax.broadcasted_iota(jnp.int32, (8, 128), 1)
    first = up[:, :128] - jnp.where(lane == 0, below, down[:, :128])
    last = jnp.where(lane == 127, above, up[:, 384:]) - down[:, 384:]
    return jnp.concatenate([first, up[:, 128:384] - down[:, 128:384], last], 1)


def wall_stress(velocity):
    x, y, z = velocity
    nu = 0.05 + 0.04 * jnp.sqrt(0.5 * z * z + 0.25 * (x * x + y * y))
    return {4: -0.5 * nu * x, 5: -0.5 * nu * y, 2: -nu * z}


def differences(field, plane, row):
    here = pl.ds(row, 8)
    center = [field[c, plane, here, :] for c in range(3)]
    along_x = [field[c, plane + 1, here, :] - field[c, plane - 1, here, :] for c in range(3)]
    along_y = [field[c, plane, pl.ds(row + 1, 8), :] - field[c, plane, pl.ds(row - 1, 8), :] for c in range(3)]
    along_z = [shift_z(center[c]) for c in range(3)]
    return center, (along_x, along_y, along_z)


def stress_rows(field, plane, tau, tau_plane, row):
    _, d = differences(field, plane, row)
    xy, xz, yz = d[0][1] + d[1][0], d[0][2] + d[2][0], d[1][2] + d[2][1]
    diagonal = d[0][0] * d[0][0] + d[1][1] * d[1][1] + d[2][2] * d[2][2]
    mixed = xy * xy + xz * xz + yz * yz
    nu = 0.05 + 0.04 * jnp.sqrt(0.5 * diagonal + 0.25 * mixed)
    half = -0.5 * nu
    rows = pl.ds(row, 8)
    for c in range(3):
        tau[c, tau_plane, rows, :] = -nu * d[c][c]
    tau[3, tau_plane, rows, :] = half * xy
    tau[4, tau_plane, rows, :] = half * xz
    tau[5, tau_plane, rows, :] = half * yz


def step_rows(field, plane, tau, tau_plane, row):
    center, d = differences(field, plane, row)
    here = pl.ds(row, 8)

    def tau_x(c):
        return tau[c, tau_plane + 1, here, :] - tau[c, tau_plane - 1, here, :]

    def tau_y(c):
        return tau[c, tau_plane, pl.ds(row + 1, 8), :] - tau[c, tau_plane, pl.ds(row - 1, 8), :]

    below = wall_stress([value[:, :128] for value in center])
    above = wall_stress([-value[:, 384:] for value in center])

    def tau_z(c):
        return shift_z(tau[c, tau_plane, here, :], below[c], above[c])

    parts = ((0, 3, 4), (3, 1, 5), (4, 5, 2))
    out = []
    for j in range(3):
        a, b, c = parts[j]
        total = tau_x(a) + tau_y(b) + tau_z(c)
        total += center[0] * d[0][j] + center[1] * d[1][j] + center[2] * d[2][j]
        new = center[j] - 0.05 * total
        out.append(new + 0.005 if j == 0 else new)
    return out


def add_columns(tile, tile_target, starts, weights, totals):
    w1, w2, w2t, w3, w3t = weights
    g1, g2, g3 = totals
    columns, targets = [], []
    for n, first in enumerate(starts):
        start = first + 127
        base_lane = pl.multiple_of(lax.shift_right_logical(start, 7) * 128, 128)
        turn = (512 - (start & 127)) & 511
        window = pltpu.roll(tile[n * 32 : n * 32 + 32, pl.ds(base_lane, 512)], turn, 1)
        columns.append(jnp.concatenate([window[:, 0:256], window[:, 1:257], window[:, 2:258]], 0))
        target = pltpu.roll(tile_target[n * 16 : n * 16 + 16, pl.ds(base_lane, 512)], (turn - 1) & 511, 1)
        targets.append(target[:, 0:256])
    half = len(starts) // 2
    cols = [jnp.concatenate(columns[:half], 1), jnp.concatenate(columns[half:], 1)]
    target = jnp.concatenate([jnp.concatenate(targets[:half], 1), jnp.concatenate(targets[half:], 1)], 0)
    h1 = jnp.concatenate([dot(w1[...], cols[0]), dot(w1[...], cols[1])], 0)
    t1 = jnp.tanh(h1)
    q1 = h1 * t1
    a1 = (h1 + q1).astype(bf16)
    s1 = (1.0 + t1) * (1.0 + (h1 - q1))
    h2 = dot(w2[...], a1)
    t2 = jnp.tanh(h2)
    q2 = h2 * t2
    a2 = (h2 + q2).astype(bf16)
    s2 = (1.0 + t2) * (1.0 + (h2 - q2))
    misfit = (dot(w3[...], a2) - target.astype(f32)).astype(bf16)
    b2 = (dot(w3t[...], misfit) * s2).astype(bf16)
    b1 = (dot(w2t[...], b2) * s1).astype(bf16)
    g3[...] += dot_cells(side_by_side(misfit), side_by_side(a2))
    both = dot_cells(b2, a1)
    g2[...] += both[0:64, 0:64] + both[64:128, 64:128]
    g1[...] += dot_cells(side_by_side(b1), jnp.concatenate(cols, 1))


def side_by_side(value):
    half = value.shape[0] // 2
    return jnp.concatenate([value[:half], value[half:]], 1)


def input_rows(field, plane):
    rows = [field[c, plane + ox - 1, 8:32, 0:512] for c in range(3) for ox in range(3)]
    return jnp.concatenate(rows, 0).astype(bf16)


def target_rows(tau, plane):
    return jnp.concatenate([tau[c, plane, 12:28, 0:512].astype(bf16) for c in range(6)], 0)


def gather(tile, at, table, rows):
    tile[at : at + table.shape[0], 128:640] = dot(table, rows).astype(bf16)


def clear_edges(*tiles):
    for tile in tiles:
        edge = jnp.zeros((tile.shape[0], 128), bf16)
        tile[:, 0:128] = edge
        tile[:, 640:768] = edge


def clear_rest(field):
    strip = jnp.zeros((8, LANES), f32)
    for c in range(3):
        for p in range(field.shape[1]):
            field[c, p, 4:12, :] = strip
            field[c, p, 28:36, :] = strip


def twice(block):
    zero = jnp.zeros_like(block)
    return jnp.concatenate([jnp.concatenate([block, zero], 1), jnp.concatenate([zero, block], 1)], 0)


def interior_kernel(
    offs, own, first, mid, last, table, packed_weights, packed_totals, field, tau, tile, tile_target,
    local_table, local_first, local_mid, local_last, sems,
):
    pairs_in = ((first, local_first), (mid, local_mid), (last, local_last), (table, local_table))
    copies = [pltpu.make_async_copy(a, b, sems.at[k]) for k, (a, b) in enumerate(pairs_in)]
    for copy in copies:
        copy.start()
    clear_edges(tile, tile_target)
    clear_rest(field)
    for c in range(3):
        for p in range(4):
            field[c, p, 12:28, 0:512] = own[c, p]
    for copy in copies:
        copy.wait()
    first, mid, last = local_first, local_mid, local_last
    pick, pick_target, order = table_parts(local_table)
    weights, totals = weight_parts(packed_weights), total_parts(packed_totals)
    w1, w2, w2t, w3, w3t = weights
    rows, cols = lax.broadcasted_iota(jnp.int32, (64, 64), 0), lax.broadcasted_iota(jnp.int32, (64, 64), 1)
    half = jnp.where(rows == cols, 0.5, 0.0).astype(bf16)
    w1[...] = (0.5 * dot(first[...], order[...])).astype(bf16)
    w2[...] = twice(0.5 * mid[...].astype(f32)).astype(bf16)
    w2t[...] = twice(dot_cells(half, mid[...])).astype(bf16)
    last_rows = jnp.concatenate([last[...].astype(f32), jnp.zeros((10, 64), f32)], 0)
    w3[...] = twice(last_rows).astype(bf16)
    w3t[...] = twice(dot_cells(half, last_rows.astype(bf16))).astype(bf16)
    packed_totals[...] = jnp.zeros_like(packed_totals)

    starts = []
    for n in range(2):
        x = n + 1
        for row in (12, 20):
            stress_rows(field, x, tau, n, row)
        gather(tile, 448 * n, pick.ref[32:480, :], input_rows(field, x))
        gather(tile_target, 224 * n, pick_target.ref[528:752, 0:96], target_rows(tau, n))
        starts += [offs[x, y] for y in range(1, 15)]
    add_columns(tile, tile_target, starts, weights, totals)


def split_bf16(value):
    high = value.astype(bf16)
    return high, (value - high.astype(f32)).astype(bf16)


FAR_FIRST = {"px": False, "py": True}


def in_order(axis, step, first, second):
    odd = (lax.axis_index(axis) + (0 if FAR_FIRST[axis] else 1)) % 2

    @pl.when(odd == 0)
    def _():
        step(first, second)

    @pl.when(odd == 1)
    def _():
        step(second, first)


def pack_x_kernel(own, first, second):
    def pack(down, up):
        for c in range(3):
            for x in range(4):
                high, rest = split_bf16(own[c, x])
                up[c, x] = high
                down[c, x + 1] = high
                if x == 3:
                    up[c, 4] = rest
                if x == 0:
                    down[c, 0] = rest

    in_order("px", pack, first, second)


def pack_y_kernel(own, x_first, x_second, first, second):
    def pack(x_low, x_high, left, right):
        for c in range(3):
            for out, at_top in ((right, True), (left, False)):

                def rows(p, count):
                    plane = x_low[c, p] if p < 4 else own[c, p - 4] if p < 8 else x_high[c, p - 7]
                    return plane.astype(f32)[16 - count :] if at_top else plane.astype(f32)[:count]

                def rest(p):
                    if p == 3 or p == 8:
                        plane = (x_low[c, 4] if p == 3 else x_high[c, 0]).astype(f32)
                    else:
                        plane = split_bf16(own[c, p - 4])[1].astype(f32)
                    return plane[15:] if at_top else plane[:1]

                blocks = [[rows(p, 4)] for p in range(4, 8)]
                blocks += [[rows(3, 3), rows(1, 1)], [rows(8, 3), rows(10, 1)], [rows(2, 2), rows(9, 2)]]
                blocks += [[rest(p) for p in range(3, 7)], [rest(7), rest(8), jnp.zeros((2, 512), f32)]]
                for k, block in enumerate(blocks):
                    out[c, k] = jnp.concatenate(block, 0).astype(bf16)

    def with_x(x_low, x_high):
        in_order("py", lambda left, right: pack(x_low, x_high, left, right), first, second)

    in_order("px", with_x, x_first, x_second)


def x_plane(x_low, own, x_high, c, p):
    if p < 4:
        plane = x_low[c, p].astype(f32)
        return plane + x_low[c, 4].astype(f32) if p == 3 else plane
    if p < 8:
        return own[c, p - 4]
    plane = x_high[c, p - 7].astype(f32)
    return plane + x_high[c, 0].astype(f32) if p == 8 else plane


def side_kernel(
    offs, own, x_first, x_second, packed_weights, before, table, packed_totals, field, tau, tile, tile_target,
    local_table, sems,
):
    copy = pltpu.make_async_copy(table, local_table, sems.at[0])
    copy.start()
    pick, pick_target, _ = table_parts(local_table)
    weights, totals = weight_parts(packed_weights), total_parts(packed_totals)
    packed_totals[...] = before[...]
    clear_edges(tile, tile_target)
    clear_rest(field)

    def place(x_low, x_high):
        for c in range(3):
            for p in range(6):
                field[c, p, 12:28, 0:512] = x_plane(x_low, own, x_high, c, p + 3)

    in_order("px", place, x_first, x_second)
    copy.wait()

    starts = []
    for n in range(2):
        x = 3 * n
        for row in (12, 20):
            stress_rows(field, x + 1, tau, n, row)
        gather(tile, 448 * n, pick.ref[32:480, :], input_rows(field, x + 1))
        gather(tile_target, 224 * n, pick_target.ref[528:752, 0:96], target_rows(tau, n))
        starts += [offs[x, y] for y in range(1, 15)]
    add_columns(tile, tile_target, starts, weights, totals)


def middle_kernel(
    offs, own, x_first, x_second, y_first, y_second,
    packed_weights, before, table, middle, packed, field, tau, tile, tile_target,
    local_table, sems, packed_totals,
):
    copy = pltpu.make_async_copy(table, local_table, sems.at[0])
    copy.start()
    pick, pick_target, order = table_parts(local_table)
    weights, totals = weight_parts(packed_weights), total_parts(packed_totals)
    packed_totals[...] = before[...]
    edges, edges_target = edge_parts(local_table)
    g1, g2, g3 = totals
    clear_edges(tile, tile_target)
    clear_rest(field)
    line = jnp.zeros((1, LANES), f32)
    for c in range(6):
        for p in range(10):
            tau[c, p, 7:8, :] = line
            tau[c, p, 32:33, :] = line
    def place_x(x_low, x_high):
        for c in range(3):
            for p in range(12):
                field[c, p, 12:28, 0:512] = x_plane(x_low, own, x_high, c, p)

    def place_y(y_low, y_high):
        parts = [(p, 4, p - 4, 0) for p in range(4, 8)]
        parts += [(3, 3, 4, 0), (1, 1, 4, 3), (8, 3, 5, 0), (10, 1, 5, 3), (2, 2, 6, 0), (9, 2, 6, 2)]
        for c in range(3):
            for p, count, k, at in parts:
                low = y_low[c, k].astype(f32)[at : at + count]
                high = y_high[c, k].astype(f32)[at : at + count]
                field[c, p, 12 - count : 12, 0:512] = low
                field[c, p, 28 : 28 + count, 0:512] = high
                if 3 <= p <= 8:
                    k, at = 7 + (p - 3) // 4, (p - 3) % 4
                    field[c, p, 11:12, 0:512] = low[count - 1 :] + y_low[c, k].astype(f32)[at : at + 1]
                    field[c, p, 28:29, 0:512] = high[:1] + y_high[c, k].astype(f32)[at : at + 1]

    in_order("px", place_x, x_first, x_second)
    in_order("py", place_y, y_first, y_second)

    def stress_zero(p, _):
        for row in (8, 16, 24):
            stress_rows(field, p + 1, tau, p, row)
        return 0

    lax.fori_loop(0, 10, stress_zero, 0, unroll=5)

    def advance_middle(p, _):
        for row in (8, 16, 24):
            new = step_rows(field, p + 2, tau, p + 1, row)
            for c in range(3):
                middle[c, p, pl.ds(row, 8), :] = new[c]
        return 0

    lax.fori_loop(0, 8, advance_middle, 0, unroll=4)
    copy.wait()

    def step(x, _):
        gather(tile, 512, edges[...], input_rows(field, x + 4))
        gather(tile_target, 256, edges_target[...], target_rows(tau, x + 3))
        for row in (12, 20):
            stress_rows(middle, x + 2, tau, 0, row)
        gather(tile, 0, pick[...], input_rows(middle, x + 2))
        gather(tile_target, 0, pick_target[...], target_rows(tau, 0))
        starts = [offs[x, y] for y in range(16)] + [offs[x, 0], offs[x, 15]]
        add_columns(tile, tile_target, starts, weights, totals)
        return 0

    lax.fori_loop(0, 4, step, 0)
    scale = 0.5**22
    ordered = lax.dot_general(
        g1[...], order[...].astype(f32), NT, preferred_element_type=f32, precision=lax.Precision.HIGHEST
    )
    mids = g2[...]
    packed[0:64, :] = scale * jnp.concatenate([ordered, jnp.zeros((64, 15), f32), mids[:, 0:32]], 1)
    packed[64:80, :] = scale * jnp.concatenate([mids[16 * k : 16 * k + 16, 32:64] for k in range(4)], 1)
    packed[80:88, :] = scale * jnp.concatenate([g3[...][0:8], jnp.zeros((8, 64), f32)], 1)


def final_kernel(middle, final, tau):
    def stress_one(p, _):
        for row in (8, 16, 24):
            stress_rows(middle, p + 1, tau, p, row)
        return 0

    lax.fori_loop(0, 6, stress_one, 0, unroll=3)

    def advance_final(p, _):
        for row in (12, 20):
            new = step_rows(middle, p + 2, tau, p + 1, row)
            for c in range(3):
                final[c, p, row - 12 : row - 4, :] = new[c]
        return 0

    lax.fori_loop(0, 4, advance_final, 0, unroll=2)


def last_sum_kernel(a, b, c, d, first, mid, last):
    total = (a[...] + b[...]) + (c[...] + d[...])
    first[...] = total[0:64, 0:81]
    rest = jnp.concatenate([total[64:80, 32 * k : 32 * k + 32] for k in range(4)], 0)
    mid[...] = jnp.concatenate([total[0:64, 96:128], rest], 1)
    last[...] = total[80:86, 0:64]


def shaped(*dims, kind=f32):
    return jax.ShapeDtypeStruct(dims, kind)


WEIGHTS, TOTALS = shaped(480, 128, kind=bf16), shaped(144, 128)


def call(kernel, args, out_shape, scratch, smem=0, us=1, mib=16, hbm=0):
    vmem = pl.BlockSpec(memory_space=pltpu.VMEM)
    scalar = pl.BlockSpec(memory_space=pltpu.SMEM)
    far = pl.BlockSpec(memory_space=pltpu.HBM)
    return pl.pallas_call(
        kernel,
        in_specs=[scalar] * smem + [vmem] * (len(args) - smem - hbm) + [far] * hbm,
        out_specs=[vmem] * len(out_shape),
        out_shape=out_shape,
        scratch_shapes=scratch,
        compiler_params=pltpu.CompilerParams(vmem_limit_bytes=mib * 2**20),
        cost_estimate=pl.CostEstimate(flops=int(us * 1.15e9), bytes_accessed=int(us * 3.69e6), transcendentals=0),
    )(*args)


def columns_scratch(planes, stress_planes, columns):
    return [
        pltpu.VMEM((3, planes, ROWS, LANES), f32),
        pltpu.VMEM((6, stress_planes, ROWS, LANES), f32),
        pltpu.VMEM((32 * columns, 768), bf16),
        pltpu.VMEM((16 * columns, 768), bf16),
        pltpu.VMEM((960, 216), bf16),
    ]


def pairs(move):
    return [(i * 16 + j, (move(i, j)[0] % 8) * 16 + move(i, j)[1] % 16) for i in range(8) for j in range(16)]


EXCHANGES = (lambda k: k ^ 1, lambda k: k ^ 3, lambda k: k ^ 2)


def along_y(turn):
    return lambda i, j: (i & 4 | turn(i & 3), j)


def along_x(turn):
    return lambda i, j: (i, j & 9 | turn(j >> 1 & 3) << 1)


def along_z(turn):
    def move(i, j):
        z = turn((j >> 3) * 2 + (i >> 2))
        return ((z & 1) * 4 + (i & 3), (z >> 1) * 8 + (j & 7))

    return move


def send(value, move):
    return lax.ppermute(value, AXES, pairs(move))


def body(velocity, first_weight, mid_weight, last_weight, offsets):
    table = jnp.asarray(selections(), bf16)
    near_x, far_x = lambda i, j: (i ^ 1, j), lambda i, j: (i + 2 * (i % 2) - 1, j)
    near_y, far_y = lambda i, j: (i, j ^ 1), lambda i, j: (i, j + 2 * (j % 2) - 1)
    to_near, to_far = call(pack_x_kernel, (velocity,), [shaped(3, 5, 16, 512, kind=bf16)] * 2, [])
    x_first, x_second = send(to_near, near_x), send(to_far, far_x)
    weights, totals = call(
        interior_kernel,
        (offsets, velocity, first_weight, mid_weight, last_weight, table),
        [WEIGHTS, TOTALS], columns_scratch(4, 2, 28)
        + [pltpu.VMEM(n, bf16) for n in ((64, 81), (64, 64), (6, 64))] + [pltpu.SemaphoreType.DMA((4,))],
        1, 6, 28, 4,
    )
    x_first, x_second, totals = lax.optimization_barrier((x_first, x_second, totals))
    to_far, to_near = call(
        pack_y_kernel, (velocity, x_first, x_second), [shaped(3, 9, 4, 512, kind=bf16)] * 2, []
    )
    y_first, y_second = send(to_far, far_y), send(to_near, near_y)
    (totals,) = call(
        side_kernel,
        (offsets, velocity, x_first, x_second, weights, totals, table),
        [TOTALS], columns_scratch(6, 2, 28) + [pltpu.SemaphoreType.DMA((1,))], 1, 6, 28, 1,
    )
    middle, packed = call(
        middle_kernel,
        (offsets, velocity, x_first, x_second, y_first, y_second, weights, totals, table),
        [shaped(3, 8, ROWS, LANES), shaped(88, 128)],
        columns_scratch(12, 10, 18) + [pltpu.SemaphoreType.DMA((1,)), pltpu.VMEM(TOTALS.shape, f32)], 1, 16, 32, 1,
    )
    (final,) = call(final_kernel, (middle,), [shaped(3, 4, 16, 512)], [pltpu.VMEM((6, 6, ROWS, LANES), f32)], 0, 3)

    packed = packed + send(packed, near_y)
    for along in (along_y, along_x):
        a, b, c = (send(packed, along(turn)) for turn in EXCHANGES)
        packed = (packed + a) + (b + c)
    a, b, c = (send(packed, along_z(turn)) for turn in EXCHANGES)
    grads = call(last_sum_kernel, (packed, a, b, c), [shaped(64, 81), shaped(64, 64), shaped(6, 64)], [])
    return final, *grads


def solution(mesh):
    in_specs = (P(None, "px", "py", None), P(), P(), P(), P("px", "py"))
    out_specs = (P(None, "px", "py", None), P(), P(), P())
    return jax.shard_map(body, mesh=mesh, in_specs=in_specs, out_specs=out_specs, check_vma=False)
```

```python
import jax
import jax.numpy as jnp
import numpy as np
from jax import lax
from jax.experimental import pallas as pl
from jax.experimental.pallas import tpu as pltpu
from jax.sharding import PartitionSpec as P

f32, bf16 = jnp.float32, jnp.bfloat16
AXES = ("px", "py")
LANES = 512
ROWS = 40
NT = (((1,), (1,)), ((), ()))


def selections():
    table = np.zeros((960, 216), np.float32)
    for y in range(16):
        for c in range(3):
            for ox in range(3):
                for oy in range(3):
                    table[y * 32 + c * 9 + ox * 3 + oy, (c * 3 + ox) * 24 + y + oy + 3] = 1
        for c in range(6):
            table[512 + y * 16 + c, c * 16 + y] = 1
    for oz in range(3):
        for c in range(3):
            for o in range(9):
                table[768 + c * 27 + o * 3 + oz, oz * 32 + c * 9 + o] = 1
    table[864:928] = table[np.r_[0:32, 480:512]]
    table[928:960] = table[np.r_[512:528, 752:768]]
    return table


class Part:
    def __init__(self, ref, first, last, lanes):
        self.ref, self.first, self.last, self.lanes = ref, first, last, lanes

    def __getitem__(self, _):
        return self.ref[self.first : self.last, 0 : self.lanes]

    def __setitem__(self, _, value):
        self.ref[self.first : self.last, 0 : self.lanes] = value


def table_parts(table):
    return Part(table, 0, 512, 216), Part(table, 512, 768, 96), Part(table, 768, 864, 96)


def edge_parts(table):
    return Part(table, 864, 928, 216), Part(table, 928, 960, 96)


def weight_parts(packed):
    return (Part(packed, 0, 64, 96), Part(packed, 64, 192, 128), Part(packed, 192, 320, 128),
            Part(packed, 320, 352, 128), Part(packed, 352, 480, 32))


def total_parts(packed):
    return Part(packed, 0, 64, 96), Part(packed, 64, 128, 64), Part(packed, 128, 144, 64)


def dot(a, b):
    return jnp.dot(a, b, preferred_element_type=f32)


def dot_cells(a, b):
    return lax.dot_general(a, b, NT, preferred_element_type=f32)


def shift_z(value, below=0.0, above=0.0):
    up, down = pltpu.roll(value, LANES - 1, 1), pltpu.roll(value, 1, 1)
    lane = lax.broadcasted_iota(jnp.int32, (8, 128), 1)
    first = up[:, :128] - jnp.where(lane == 0, below, down[:, :128])
    last = jnp.where(lane == 127, above, up[:, 384:]) - down[:, 384:]
    return jnp.concatenate([first, up[:, 128:384] - down[:, 128:384], last], 1)


def wall_stress(velocity):
    x, y, z = velocity
    nu = 0.05 + 0.04 * jnp.sqrt(0.5 * z * z + 0.25 * (x * x + y * y))
    return {4: -0.5 * nu * x, 5: -0.5 * nu * y, 2: -nu * z}


def differences(field, plane, row):
    here = pl.ds(row, 8)
    center = [field[c, plane, here, :] for c in range(3)]
    along_x = [field[c, plane + 1, here, :] - field[c, plane - 1, here, :] for c in range(3)]
    along_y = [field[c, plane, pl.ds(row + 1, 8), :] - field[c, plane, pl.ds(row - 1, 8), :] for c in range(3)]
    along_z = [shift_z(center[c]) for c in range(3)]
    return center, (along_x, along_y, along_z)


def stress_rows(field, plane, tau, tau_plane, row):
    _, d = differences(field, plane, row)
    xy, xz, yz = d[0][1] + d[1][0], d[0][2] + d[2][0], d[1][2] + d[2][1]
    diagonal = d[0][0] * d[0][0] + d[1][1] * d[1][1] + d[2][2] * d[2][2]
    mixed = xy * xy + xz * xz + yz * yz
    nu = 0.05 + 0.04 * jnp.sqrt(0.5 * diagonal + 0.25 * mixed)
    half = -0.5 * nu
    rows = pl.ds(row, 8)
    for c in range(3):
        tau[c, tau_plane, rows, :] = -nu * d[c][c]
    tau[3, tau_plane, rows, :] = half * xy
    tau[4, tau_plane, rows, :] = half * xz
    tau[5, tau_plane, rows, :] = half * yz


def step_rows(field, plane, tau, tau_plane, row):
    center, d = differences(field, plane, row)
    here = pl.ds(row, 8)

    def tau_x(c):
        return tau[c, tau_plane + 1, here, :] - tau[c, tau_plane - 1, here, :]

    def tau_y(c):
        return tau[c, tau_plane, pl.ds(row + 1, 8), :] - tau[c, tau_plane, pl.ds(row - 1, 8), :]

    below = wall_stress([value[:, :128] for value in center])
    above = wall_stress([-value[:, 384:] for value in center])

    def tau_z(c):
        return shift_z(tau[c, tau_plane, here, :], below[c], above[c])

    parts = ((0, 3, 4), (3, 1, 5), (4, 5, 2))
    out = []
    for j in range(3):
        a, b, c = parts[j]
        total = tau_x(a) + tau_y(b) + tau_z(c)
        total += center[0] * d[0][j] + center[1] * d[1][j] + center[2] * d[2][j]
        new = center[j] - 0.05 * total
        out.append(new + 0.005 if j == 0 else new)
    return out


def add_columns(tile, tile_target, starts, weights, totals):
    w1, w2, w2t, w3, w3t = weights
    g1, g2, g3 = totals
    columns, targets = [], []
    for n, first in enumerate(starts):
        start = first + 127
        base_lane = pl.multiple_of(lax.shift_right_logical(start, 7) * 128, 128)
        turn = (512 - (start & 127)) & 511
        window = pltpu.roll(tile[n * 32 : n * 32 + 32, pl.ds(base_lane, 512)], turn, 1)
        columns.append(jnp.concatenate([window[:, 0:256], window[:, 1:257], window[:, 2:258]], 0))
        target = pltpu.roll(tile_target[n * 16 : n * 16 + 16, pl.ds(base_lane, 512)], (turn - 1) & 511, 1)
        targets.append(target[:, 0:256])
    half = len(starts) // 2
    cols = [jnp.concatenate(columns[:half], 1), jnp.concatenate(columns[half:], 1)]
    target = jnp.concatenate([jnp.concatenate(targets[:half], 1), jnp.concatenate(targets[half:], 1)], 0)
    h1 = jnp.concatenate([dot(w1[...], cols[0]), dot(w1[...], cols[1])], 0)
    t1 = jnp.tanh(h1)
    q1 = h1 * t1
    a1 = (h1 + q1).astype(bf16)
    s1 = (1.0 + t1) * (1.0 + (h1 - q1))
    h2 = dot(w2[...], a1)
    t2 = jnp.tanh(h2)
    q2 = h2 * t2
    a2 = (h2 + q2).astype(bf16)
    s2 = (1.0 + t2) * (1.0 + (h2 - q2))
    misfit = (dot(w3[...], a2) - target.astype(f32)).astype(bf16)
    b2 = (dot(w3t[...], misfit) * s2).astype(bf16)
    b1 = (dot(w2t[...], b2) * s1).astype(bf16)
    g3[...] += dot_cells(side_by_side(misfit), side_by_side(a2))
    both = dot_cells(b2, a1)
    g2[...] += both[0:64, 0:64] + both[64:128, 64:128]
    g1[...] += dot_cells(side_by_side(b1), jnp.concatenate(cols, 1))


def side_by_side(value):
    half = value.shape[0] // 2
    return jnp.concatenate([value[:half], value[half:]], 1)


def input_rows(field, plane):
    rows = [field[c, plane + ox - 1, 8:32, 0:512] for c in range(3) for ox in range(3)]
    return jnp.concatenate(rows, 0).astype(bf16)


def target_rows(tau, plane):
    return jnp.concatenate([tau[c, plane, 12:28, 0:512].astype(bf16) for c in range(6)], 0)


def gather(tile, at, table, rows):
    tile[at : at + table.shape[0], 128:640] = dot(table, rows).astype(bf16)


def clear_edges(*tiles):
    for tile in tiles:
        edge = jnp.zeros((tile.shape[0], 128), bf16)
        tile[:, 0:128] = edge
        tile[:, 640:768] = edge


def clear_rest(field):
    strip = jnp.zeros((8, LANES), f32)
    for c in range(3):
        for p in range(field.shape[1]):
            field[c, p, 4:12, :] = strip
            field[c, p, 28:36, :] = strip


def twice(block):
    zero = jnp.zeros_like(block)
    return jnp.concatenate([jnp.concatenate([block, zero], 1), jnp.concatenate([zero, block], 1)], 0)


def interior_kernel(
    offs, own, last, first, mid, table, packed_weights, packed_totals, field, tau, tile, tile_target,
    local_table, local_first, local_mid, sems,
):
    pairs_in = ((first, local_first), (mid, local_mid), (table, local_table))
    copies = [pltpu.make_async_copy(a, b, sems.at[k]) for k, (a, b) in enumerate(pairs_in)]
    for copy in copies:
        copy.start()
    clear_edges(tile, tile_target)
    clear_rest(field)
    for c in range(3):
        for p in range(4):
            field[c, p, 12:28, 0:512] = own[c, p]
    for copy in copies:
        copy.wait()
    first, mid = local_first, local_mid
    pick, pick_target, order = table_parts(local_table)
    weights, totals = weight_parts(packed_weights), total_parts(packed_totals)
    w1, w2, w2t, w3, w3t = weights
    rows, cols = lax.broadcasted_iota(jnp.int32, (64, 64), 0), lax.broadcasted_iota(jnp.int32, (64, 64), 1)
    half = jnp.where(rows == cols, 0.5, 0.0).astype(bf16)
    w1[...] = (0.5 * dot(first[...], order[...].astype(f32)[0:81].astype(bf16))).astype(bf16)
    w2[...] = twice(0.5 * mid[...].astype(f32)).astype(bf16)
    w2t[...] = twice(dot_cells(half, mid[...])).astype(bf16)
    last_rows = jnp.concatenate([last[...].astype(f32), jnp.zeros((10, 64), f32)], 0)
    w3[...] = twice(last_rows).astype(bf16)
    w3t[...] = twice(dot_cells(half, last_rows.astype(bf16))).astype(bf16)
    packed_totals[...] = jnp.zeros_like(packed_totals)

    starts = []
    for n in range(2):
        x = n + 1
        for row in (12, 20):
            stress_rows(field, x, tau, n, row)
        gather(tile, 448 * n, pick.ref[32:480, :], input_rows(field, x))
        gather(tile_target, 224 * n, pick_target.ref[528:752, 0:96], target_rows(tau, n))
        starts += [offs[x, y] for y in range(1, 15)]
    add_columns(tile, tile_target, starts, weights, totals)


def split_bf16(value):
    high = value.astype(bf16)
    return high, (value - high.astype(f32)).astype(bf16)


FAR_FIRST = {"px": False, "py": True}


def in_order(axis, step, first, second):
    odd = (lax.axis_index(axis) + (0 if FAR_FIRST[axis] else 1)) % 2

    @pl.when(odd == 0)
    def _():
        step(first, second)

    @pl.when(odd == 1)
    def _():
        step(second, first)


def pack_x_kernel(own, first, second):
    def pack(down, up):
        for c in range(3):
            for x in range(4):
                high, rest = split_bf16(own[c, x])
                up[c, x] = high
                down[c, x + 1] = high
                if x == 3:
                    up[c, 4] = rest
                if x == 0:
                    down[c, 0] = rest

    in_order("px", pack, first, second)


def pack_y_kernel(own, x_first, x_second, first, second):
    def pack(x_low, x_high, left, right):
        for c in range(3):
            for out, at_top in ((right, True), (left, False)):

                def rows(p, count):
                    plane = x_low[c, p] if p < 4 else own[c, p - 4] if p < 8 else x_high[c, p - 7]
                    return plane.astype(f32)[16 - count :] if at_top else plane.astype(f32)[:count]

                def rest(p):
                    if p == 3 or p == 8:
                        plane = (x_low[c, 4] if p == 3 else x_high[c, 0]).astype(f32)
                    else:
                        plane = split_bf16(own[c, p - 4])[1].astype(f32)
                    return plane[15:] if at_top else plane[:1]

                blocks = [[rows(p, 4)] for p in range(4, 8)]
                blocks += [[rows(3, 3), rows(1, 1)], [rows(8, 3), rows(10, 1)], [rows(2, 2), rows(9, 2)]]
                blocks += [[rest(p) for p in range(3, 7)], [rest(7), rest(8), jnp.zeros((2, 512), f32)]]
                for k, block in enumerate(blocks):
                    out[c, k] = jnp.concatenate(block, 0).astype(bf16)

    def with_x(x_low, x_high):
        in_order("py", lambda left, right: pack(x_low, x_high, left, right), first, second)

    in_order("px", with_x, x_first, x_second)


def x_plane(x_low, own, x_high, c, p):
    if p < 4:
        plane = x_low[c, p].astype(f32)
        return plane + x_low[c, 4].astype(f32) if p == 3 else plane
    if p < 8:
        return own[c, p - 4]
    plane = x_high[c, p - 7].astype(f32)
    return plane + x_high[c, 0].astype(f32) if p == 8 else plane


def side_kernel(
    offs, own, x_first, x_second, packed_weights, before, table, packed_totals, field, tau, tile, tile_target,
    local_table, sems,
):
    copy = pltpu.make_async_copy(table, local_table, sems.at[0])
    copy.start()
    pick, pick_target, _ = table_parts(local_table)
    weights, totals = weight_parts(packed_weights), total_parts(packed_totals)
    packed_totals[...] = before[...]
    clear_edges(tile, tile_target)
    clear_rest(field)

    def place(x_low, x_high):
        for c in range(3):
            for p in range(6):
                field[c, p, 12:28, 0:512] = x_plane(x_low, own, x_high, c, p + 3)

    in_order("px", place, x_first, x_second)
    copy.wait()

    starts = []
    for n in range(2):
        x = 3 * n
        for row in (12, 20):
            stress_rows(field, x + 1, tau, n, row)
        gather(tile, 448 * n, pick.ref[32:480, :], input_rows(field, x + 1))
        gather(tile_target, 224 * n, pick_target.ref[528:752, 0:96], target_rows(tau, n))
        starts += [offs[x, y] for y in range(1, 15)]
    add_columns(tile, tile_target, starts, weights, totals)


def middle_kernel(
    offs, own, x_first, x_second, y_first, y_second,
    packed_weights, before, table, middle, packed, field, tau, tile, tile_target,
    local_table, sems, packed_totals,
):
    copy = pltpu.make_async_copy(table, local_table, sems.at[0])
    copy.start()
    pick, pick_target, order = table_parts(local_table)
    weights, totals = weight_parts(packed_weights), total_parts(packed_totals)
    packed_totals[...] = before[...]
    edges, edges_target = edge_parts(local_table)
    g1, g2, g3 = totals
    clear_edges(tile, tile_target)
    clear_rest(field)
    line = jnp.zeros((1, LANES), f32)
    for c in range(6):
        for p in range(10):
            tau[c, p, 7:8, :] = line
            tau[c, p, 32:33, :] = line
    def place_x(x_low, x_high):
        for c in range(3):
            for p in range(12):
                field[c, p, 12:28, 0:512] = x_plane(x_low, own, x_high, c, p)

    def place_y(y_low, y_high):
        parts = [(p, 4, p - 4, 0) for p in range(4, 8)]
        parts += [(3, 3, 4, 0), (1, 1, 4, 3), (8, 3, 5, 0), (10, 1, 5, 3), (2, 2, 6, 0), (9, 2, 6, 2)]
        for c in range(3):
            for p, count, k, at in parts:
                low = y_low[c, k].astype(f32)[at : at + count]
                high = y_high[c, k].astype(f32)[at : at + count]
                field[c, p, 12 - count : 12, 0:512] = low
                field[c, p, 28 : 28 + count, 0:512] = high
                if 3 <= p <= 8:
                    k, at = 7 + (p - 3) // 4, (p - 3) % 4
                    field[c, p, 11:12, 0:512] = low[count - 1 :] + y_low[c, k].astype(f32)[at : at + 1]
                    field[c, p, 28:29, 0:512] = high[:1] + y_high[c, k].astype(f32)[at : at + 1]

    in_order("px", place_x, x_first, x_second)
    in_order("py", place_y, y_first, y_second)

    def stress_zero(p, _):
        for row in (8, 16, 24):
            stress_rows(field, p + 1, tau, p, row)
        return 0

    lax.fori_loop(0, 10, stress_zero, 0, unroll=5)

    def advance_middle(p, _):
        for row in (8, 16, 24):
            new = step_rows(field, p + 2, tau, p + 1, row)
            for c in range(3):
                middle[c, p, pl.ds(row, 8), :] = new[c]
        return 0

    lax.fori_loop(0, 8, advance_middle, 0, unroll=4)
    copy.wait()

    def step(x, _):
        gather(tile, 512, edges[...], input_rows(field, x + 4))
        gather(tile_target, 256, edges_target[...], target_rows(tau, x + 3))
        for row in (12, 20):
            stress_rows(middle, x + 2, tau, 0, row)
        gather(tile, 0, pick[...], input_rows(middle, x + 2))
        gather(tile_target, 0, pick_target[...], target_rows(tau, 0))
        starts = [offs[x, y] for y in range(16)] + [offs[x, 0], offs[x, 15]]
        add_columns(tile, tile_target, starts, weights, totals)
        return 0

    lax.fori_loop(0, 4, step, 0)
    scale = 0.5**22
    ordered = lax.dot_general(
        g1[...], order[...].astype(f32)[0:81], NT, preferred_element_type=f32, precision=lax.Precision.HIGHEST
    )
    mids = g2[...]
    packed[0:64, :] = scale * jnp.concatenate([ordered, jnp.zeros((64, 15), f32), mids[:, 0:32]], 1)
    packed[64:80, :] = scale * jnp.concatenate([mids[16 * k : 16 * k + 16, 32:64] for k in range(4)], 1)
    packed[80:88, :] = scale * jnp.concatenate([g3[...][0:8], jnp.zeros((8, 64), f32)], 1)


def final_kernel(middle, final, tau):
    def stress_one(p, _):
        for row in (8, 16, 24):
            stress_rows(middle, p + 1, tau, p, row)
        return 0

    lax.fori_loop(0, 6, stress_one, 0, unroll=3)

    def advance_final(p, _):
        for row in (12, 20):
            new = step_rows(middle, p + 2, tau, p + 1, row)
            for c in range(3):
                final[c, p, row - 12 : row - 4, :] = new[c]
        return 0

    lax.fori_loop(0, 4, advance_final, 0, unroll=2)


def last_sum_kernel(a, b, c, d, first, mid, last):
    total = (a[...] + b[...]) + (c[...] + d[...])
    first[...] = total[0:64, 0:81]
    rest = jnp.concatenate([total[64:80, 32 * k : 32 * k + 32] for k in range(4)], 0)
    mid[...] = jnp.concatenate([total[0:64, 96:128], rest], 1)
    last[...] = total[80:86, 0:64]


def shaped(*dims, kind=f32):
    return jax.ShapeDtypeStruct(dims, kind)


WEIGHTS, TOTALS = shaped(480, 128, kind=bf16), shaped(144, 128)


def call(kernel, args, out_shape, scratch, smem=0, us=1, mib=16, hbm=0):
    vmem = pl.BlockSpec(memory_space=pltpu.VMEM)
    scalar = pl.BlockSpec(memory_space=pltpu.SMEM)
    far = pl.BlockSpec(memory_space=pltpu.HBM)
    return pl.pallas_call(
        kernel,
        in_specs=[scalar] * smem + [vmem] * (len(args) - smem - hbm) + [far] * hbm,
        out_specs=[vmem] * len(out_shape),
        out_shape=out_shape,
        scratch_shapes=scratch,
        compiler_params=pltpu.CompilerParams(vmem_limit_bytes=mib * 2**20),
        cost_estimate=pl.CostEstimate(flops=int(us * 1.15e9), bytes_accessed=int(us * 3.69e6), transcendentals=0),
    )(*args)


def columns_scratch(planes, stress_planes, columns):
    return [
        pltpu.VMEM((3, planes, ROWS, LANES), f32),
        pltpu.VMEM((6, stress_planes, ROWS, LANES), f32),
        pltpu.VMEM((32 * columns, 768), bf16),
        pltpu.VMEM((16 * columns, 768), bf16),
        pltpu.VMEM((960, 216), bf16),
    ]


def pairs(move):
    return [(i * 16 + j, (move(i, j)[0] % 8) * 16 + move(i, j)[1] % 16) for i in range(8) for j in range(16)]


EXCHANGES = (lambda k: k ^ 1, lambda k: k ^ 3, lambda k: k ^ 2)


def along_y(turn):
    return lambda i, j: (i & 4 | turn(i & 3), j)


def along_x(turn):
    return lambda i, j: (i, j & 9 | turn(j >> 1 & 3) << 1)


def along_z(turn):
    def move(i, j):
        z = turn((j >> 3) * 2 + (i >> 2))
        return ((z & 1) * 4 + (i & 3), (z >> 1) * 8 + (j & 7))

    return move


def send(value, move):
    return lax.ppermute(value, AXES, pairs(move))


def body(velocity, first_weight, mid_weight, last_weight, offsets):
    table = jnp.asarray(selections(), bf16)
    near_x, far_x = lambda i, j: (i ^ 1, j), lambda i, j: (i + 2 * (i % 2) - 1, j)
    near_y, far_y = lambda i, j: (i, j ^ 1), lambda i, j: (i, j + 2 * (j % 2) - 1)
    to_near, to_far = call(pack_x_kernel, (velocity,), [shaped(3, 5, 16, 512, kind=bf16)] * 2, [])
    x_first, x_second = send(to_near, near_x), send(to_far, far_x)
    weights, totals = call(
        interior_kernel,
        (offsets, velocity, last_weight, first_weight, mid_weight, table),
        [WEIGHTS, TOTALS], columns_scratch(4, 2, 28)
        + [pltpu.VMEM(n, bf16) for n in ((64, 81), (64, 64))] + [pltpu.SemaphoreType.DMA((3,))],
        1, 6, 28, 3,
    )
    x_first, x_second, totals = lax.optimization_barrier((x_first, x_second, totals))
    to_far, to_near = call(
        pack_y_kernel, (velocity, x_first, x_second), [shaped(3, 9, 4, 512, kind=bf16)] * 2, []
    )
    y_first, y_second = send(to_far, far_y), send(to_near, near_y)
    (totals,) = call(
        side_kernel,
        (offsets, velocity, x_first, x_second, weights, totals, table),
        [TOTALS], columns_scratch(6, 2, 28) + [pltpu.SemaphoreType.DMA((1,))], 1, 6, 28, 1,
    )
    middle, packed = call(
        middle_kernel,
        (offsets, velocity, x_first, x_second, y_first, y_second, weights, totals, table),
        [shaped(3, 8, ROWS, LANES), shaped(88, 128)],
        columns_scratch(12, 10, 18) + [pltpu.SemaphoreType.DMA((1,)), pltpu.VMEM(TOTALS.shape, f32)], 1, 16, 32, 1,
    )
    (final,) = call(final_kernel, (middle,), [shaped(3, 4, 16, 512)], [pltpu.VMEM((6, 6, ROWS, LANES), f32)], 0, 3)

    packed = packed + send(packed, near_y)
    for along in (along_y, along_x):
        a, b, c = (send(packed, along(turn)) for turn in EXCHANGES)
        packed = (packed + a) + (b + c)
    a, b, c = (send(packed, along_z(turn)) for turn in EXCHANGES)
    grads = call(last_sum_kernel, (packed, a, b, c), [shaped(64, 81), shaped(64, 64), shaped(6, 64)], [])
    return final, *grads


def solution(mesh):
    in_specs = (P(None, "px", "py", None), P(), P(), P(), P("px", "py"))
    out_specs = (P(None, "px", "py", None), P(), P(), P())
    return jax.shard_map(body, mesh=mesh, in_specs=in_specs, out_specs=out_specs, check_vma=False)
```
